256 devices in a mesh: head: 16 (over x, y_lo, core), ctx: 16 (over y_hi, z).
Axes of the slice: x: 4, y: 4 (y_hi: 2, y_lo: 2; y = y_hi * 2 + y_lo), z: 8, core: 2. Of those that a mesh axis runs over, the one named last changes fastest.
Arguments:
- queries: bfloat16 [4, 16, 256, 12288], P(None, 'ctx', 'head'), may hold values from -5 to 5
- key_vectors: bfloat16 [4, 16, 256, 1024], P(None, 'ctx', 'head'), may hold values from -5 to 5
- value_vectors: bfloat16 [4, 16, 256, 1024], P(None, 'ctx', 'head'), may hold values from -6 to 6
- grad_output: bfloat16 [4, 16, 256, 12288], P(None, 'ctx', 'head'), may hold values from -6 to 6
- doc_ids: int32 [16384], replicated, may hold values from 0 to 31, never falling along the last dimension, each value on 1 to 1024 neighbouring positions
Outputs:
- grad_queries: bfloat16 [4, 16, 256, 12288], P(None, 'ctx', 'head')
- grad_keys: bfloat16 [4, 16, 256, 1024], P(None, 'ctx', 'head')
- grad_values: bfloat16 [4, 16, 256, 1024], P(None, 'ctx', 'head')
The draws below stay inside these ranges and needn't reach their ends.
Inputs may be any that keep to these rules, and one draw needn't show every extreme that they name: `doc_ids`: document numbers never fall along the sequence; a document holds 1 to 1024 tokens.
All inputs are finite; a program needn't handle non-finite values.
Results may differ from the reference program's by a relative error of at most 0.0066.
Values may be sent and summed in bfloat16 or wider, within the bound.
A program may use at most 128 MiB of HBM per device.

```python
import math
import jax
import jax.numpy as jnp
import numpy as np
from jax import lax

HD = 128
STRIPE = 256
SPD = 4
QHEADS = 96
KVHEADS = 8
SEQ = 16384
WIN = 512
N_CTX = 16


def draw_queries(key, part):
    key = jax.random.fold_in(key, 1)
    sample = jnp.clip(jax.random.normal(key, (SEQ, QHEADS, HD), jnp.float32), -4.0, 4.0)
    return sample.reshape(SPD, N_CTX, STRIPE, QHEADS * HD).astype(jnp.bfloat16)


def draw_key_vectors(key, part):
    key = jax.random.fold_in(key, 2)
    sample = jnp.clip(jax.random.normal(key, (SEQ, KVHEADS, HD), jnp.float32), -4.0, 4.0)
    return sample.reshape(SPD, N_CTX, STRIPE, KVHEADS * HD).astype(jnp.bfloat16)


def block_scale(rng, extent, pieces, least, largest):
    factor_of = 1.0
    for axis_at, parts in pieces:
        steps = jax.random.uniform(jax.random.fold_in(jax.random.fold_in(rng, 6), axis_at), (parts,), jnp.float32, least / len(pieces), largest / len(pieces))
        factor_of = factor_of * jnp.repeat(jnp.exp(steps), extent[axis_at] // parts).reshape((-1,) + (1,) * (len(extent) - 1 - axis_at))
    return factor_of


def length_profile(count, total, bound, slope):
    weights = [(1 << 20) // math.isqrt(rank ** slope) + 1 for rank in range(2, count + 1)]
    rest, given = total - bound - (count - 1), [1] * (count - 1)
    while rest > 0:
        movable = [i for i in range(count - 1) if given[i] < bound]
        mass, left = sum([weights[i] for i in movable]), rest
        for i in movable:
            addition = min(bound - given[i], max(1, left * weights[i] // mass), rest)
            given[i] = given[i] + addition
            rest = rest - addition
    return np.array([bound] + given)


def ragged(stream_key, amount, total, limit, lean):
    if amount == 2:
        one = jax.random.randint(stream_key, (), max(1, total - limit), min(limit, total - 1) + 1)
        return jnp.stack([one, total - one])
    tallies = jnp.asarray(length_profile(amount, total, limit, lean), jnp.int32)
    twos = (amount - 1) // 2
    source_of, sink = tallies[1:1 + 2 * twos:2], tallies[2:2 + 2 * twos:2]
    margin = jnp.minimum(source_of - 1, limit - sink)
    moved = jax.random.randint(jax.random.fold_in(stream_key, 1), (twos,), 0, 1 << 20) % (margin + 1)
    tallies = tallies.at[1:1 + 2 * twos:2].set(source_of - moved).at[2:2 + 2 * twos:2].set(sink + moved)
    return tallies[jax.random.permutation(jax.random.fold_in(stream_key, 2), amount)]


def normal_values(key, shape, spread, limit, cuts=(), held_as=jnp.bfloat16):
    result = spread * jax.random.normal(key, shape, jnp.float32)
    if cuts:
        result = result * block_scale(key, shape, cuts, -0.22, 0.18)
    return jnp.clip(result, -limit, limit).astype(held_as)


def setup_inputs(seed: int = 0) -> dict:
    keys = jax.random.split(jax.random.key(seed), 6)
    queries = draw_queries(jax.random.fold_in(keys[5], 71), 0)
    key_vectors = draw_key_vectors(jax.random.fold_in(keys[5], 71), 0)
    value_vectors = normal_values(keys[2], (SPD, N_CTX, STRIPE, KVHEADS * HD), 1.0, 6.0, ((1, 16), (2, 16)))
    grad_output = normal_values(keys[3], (SPD, N_CTX, STRIPE, QHEADS * HD), 1.0, 6.0, ((1, 16), (2, 16)))
    doc_ids = jnp.searchsorted(jnp.cumsum(ragged(keys[4], SEQ // (2 * STRIPE), SEQ, 4 * STRIPE, 2)), jnp.arange(SEQ), side="right").astype(jnp.int32)
    return dict(queries=queries, key_vectors=key_vectors, value_vectors=value_vectors, grad_output=grad_output, doc_ids=doc_ids)


def rounded(value):
    return lax.optimization_barrier(value.astype(jnp.bfloat16)).astype(jnp.float32)

def stripe_grads(query_rows, grad_rows, key_rows, value_rows, allowed, factor):
    scores = jnp.einsum('qgjmd,kgd->gjmqk', query_rows, key_rows) * factor
    masked = jnp.where(allowed, scores, -jnp.inf)
    row_max = lax.optimization_barrier(jnp.max(masked, axis=-1, keepdims=True))
    exponent = jnp.where(allowed, jnp.exp(masked - row_max), 0.0)
    weights = exponent / lax.optimization_barrier(jnp.sum(exponent, axis=-1, keepdims=True))
    dweights = jnp.einsum('qgjmd,kgd->gjmqk', grad_rows, value_rows)
    row_dot = lax.optimization_barrier(jnp.sum(weights * dweights, axis=-1, keepdims=True))
    dscores = rounded(factor * weights * (dweights - row_dot))
    weight_bf = rounded(weights)
    grad_q = jnp.einsum('gjmqk,kgd->qgjmd', dscores, key_rows)
    grad_k = jnp.einsum('gjmqk,qgjmd->kgjd', dscores, query_rows)
    grad_v = jnp.einsum('gjmqk,qgjmd->kgjd', weight_bf, grad_rows)
    return (grad_q, grad_k, grad_v)

def reference(queries, key_vectors, value_vectors, grad_output, doc_ids):
    stripes = SPD * N_CTX
    kv_count = KVHEADS
    half_group = QHEADS // (2 * KVHEADS)
    factor = 1.0 / math.sqrt(HD)
    query_all = queries.reshape(stripes, STRIPE, kv_count, 2, half_group, HD)
    grad_all = grad_output.reshape(stripes, STRIPE, kv_count, 2, half_group, HD)
    key_all = key_vectors.reshape(stripes, STRIPE, kv_count, HD)
    value_all = value_vectors.reshape(stripes, STRIPE, kv_count, HD)
    pad_rows = jnp.zeros((2, STRIPE, kv_count, HD), key_vectors.dtype)
    key_padded = jnp.concatenate([pad_rows, key_all], axis=0)
    value_padded = jnp.concatenate([pad_rows, value_all], axis=0)
    doc_flat = doc_ids.astype(jnp.int32)
    doc_pad = jnp.concatenate([jnp.full((2 * STRIPE,), -1, jnp.int32), doc_flat])
    offsets = jnp.arange(STRIPE, dtype=jnp.int32)
    key_offsets = jnp.arange(3 * STRIPE, dtype=jnp.int32)

    def visit(running, stripe_at):
        key_total, value_total = running
        query_rows = lax.dynamic_index_in_dim(query_all, stripe_at, 0, keepdims=False).astype(jnp.float32)
        grad_rows = lax.dynamic_index_in_dim(grad_all, stripe_at, 0, keepdims=False).astype(jnp.float32)
        key_rows = lax.dynamic_slice_in_dim(key_padded, stripe_at, 3, 0).reshape(3 * STRIPE, kv_count, HD).astype(jnp.float32)
        value_rows = lax.dynamic_slice_in_dim(value_padded, stripe_at, 3, 0).reshape(3 * STRIPE, kv_count, HD).astype(jnp.float32)
        query_pos = stripe_at * STRIPE + offsets
        key_pos = (stripe_at - 2) * STRIPE + key_offsets
        query_doc = lax.dynamic_slice_in_dim(doc_flat, stripe_at * STRIPE, STRIPE)
        key_doc = lax.dynamic_slice_in_dim(doc_pad, stripe_at * STRIPE, 3 * STRIPE)
        distance = query_pos[:, None] - key_pos[None, :]
        allowed = (distance >= 0) & (distance < WIN) & (key_pos[None, :] >= 0) & (query_doc[:, None] == key_doc[None, :])
        grad_q, grad_k, grad_v = stripe_grads(query_rows, grad_rows, key_rows, value_rows, allowed, factor)
        key_window = lax.dynamic_slice_in_dim(key_total, stripe_at, 3, 0) + grad_k.reshape(3, STRIPE, kv_count, 2, HD)
        key_total = lax.dynamic_update_slice_in_dim(key_total, key_window, stripe_at, 0)
        value_window = lax.dynamic_slice_in_dim(value_total, stripe_at, 3, 0) + grad_v.reshape(3, STRIPE, kv_count, 2, HD)
        value_total = lax.dynamic_update_slice_in_dim(value_total, value_window, stripe_at, 0)
        return ((key_total, value_total), grad_q.astype(jnp.bfloat16))
    empty_total = jnp.zeros((stripes + 2, STRIPE, kv_count, 2, HD), jnp.float32)
    (key_total, value_total), grad_all_q = lax.scan(visit, (empty_total, empty_total), jnp.arange(stripes, dtype=jnp.int32))

    def pair_sum(total):
        halves = rounded(total[2:])
        return lax.optimization_barrier(jnp.sum(halves, axis=3)).astype(jnp.bfloat16).reshape(SPD, N_CTX, STRIPE, kv_count * HD)
    grad_queries = grad_all_q.reshape(SPD, N_CTX, STRIPE, QHEADS * HD)
    return (grad_queries, pair_sum(key_total), pair_sum(value_total))
```

```python
import functools
import math

import jax
import jax.numpy as jnp
from jax import lax
from jax.experimental import pallas as pl
from jax.experimental.pallas import tpu as pltpu
from jax.sharding import PartitionSpec as P

MESH = pl.DeviceIdType.MESH
HD = 128
NX = 4
NJ = 8
NCTX = 16
SLOTS = 4
ROWS = 16
GRP = 32
HPG = 12
QW = HPG * HD
NKEY = 17 * GRP
STACK = HPG * GRP
LOG2E = 1.4426950408889634
FACTOR = 1.0 / math.sqrt(HD)
PEERS = tuple((dx, dc) for dx in (2, 1, 3, 0) for dc in (0, 1) if (dx, dc) != (0, 0))


def kernel(
    q_ref, k_ref, v_ref, g_ref, doc_ref, dq_ref, dk_ref, dv_ref,
    qr, gr, dqs, kv, qc, gc, kc, vc, bias, start, acc, dks, dko, rx, home,
    q_ss, q_rs, a_ss, a_rs, f_ss, f_rs, dq_ss, dq_rs, dk_ss, dk_rs, h_ss, h_rs,
):
    head = lax.axis_index("head")
    c = lax.axis_index("ctx")
    x, y, core = head // 4, (head // 2) % 2, head % 2
    me = x * 2 + core
    other = 1 - y

    def dev(nj, ny, nc):
        return dict(head=(nj // 2) * 4 + ny * 2 + nj % 2, ctx=nc)

    def hop(by):
        return (c + by + NCTX) % NCTX

    def peer(dx, dc):
        return ((x + dx) % NX) * 2 + (core + dc) % 2

    def remote(src, dst, ss, rs, to):
        return pltpu.make_async_remote_copy(
            src_ref=src, dst_ref=dst, send_sem=ss, recv_sem=rs, device_id=to, device_id_type=MESH
        )

    def arrived(ref, sem):
        pltpu.make_async_copy(ref, ref, sem).wait()

    barrier = pltpu.get_barrier_semaphore()
    partners = [dev(peer(*p), y, c) for p in PEERS] + [dev(me, other, c)]
    partners += [dev(me, ny, hop(b)) for b in (1, 2, -1, -2) for ny in (y, other)]
    for to in partners:
        pl.semaphore_signal(barrier, inc=1, device_id=to, device_id_type=MESH)
    pl.semaphore_wait(barrier, len(partners))

    def kv_src(ref, j):
        return ref.at[:, 0, :, pl.ds(pl.multiple_of(j * HD, HD), HD)]

    def kv_dst(n, j):
        return kv.at[n, :, 2, j // 2, y, pl.ds(pl.multiple_of((j % 2) * ROWS, ROWS), ROWS)]

    for p in PEERS:
        j = peer(*p)
        for n, ref in enumerate((k_ref, v_ref)):
            remote(kv_src(ref, j), kv_dst(n, me), a_ss.at[n, j], a_rs.at[n, me], dev(j, y, c)).start()
    for n, ref in enumerate((k_ref, v_ref)):
        pltpu.make_async_copy(kv_src(ref, me), kv_dst(n, me), a_rs.at[n, me]).start()

    def q_src(ref, a, j):
        return ref.at[a, 0, :, pl.ds(pl.multiple_of(j * QW, QW), QW)]

    def send_q(a):
        for p in PEERS:
            j = peer(*p)
            for n, (ref, to) in enumerate(((q_ref, qr), (g_ref, gr))):
                remote(q_src(ref, a, j), to.at[a, me], q_ss.at[n, a, j], q_rs.at[n, a, me], dev(j, y, c)).start()
        for n, (ref, to) in enumerate(((q_ref, qr), (g_ref, gr))):
            pltpu.make_async_copy(q_src(ref, a, me), to.at[a, me], q_rs.at[n, a, me]).start()

    send_q(0)

    doc = doc_ref[...]
    row = lax.broadcasted_iota(jnp.int32, doc.shape, 0)
    lane = lax.broadcasted_iota(jnp.int32, doc.shape, 1)
    before = pltpu.roll(doc, 1, 1)
    before = jnp.where(lane == 0, pltpu.roll(before, 1, 0), before)
    run = jnp.where(doc != before, row * HD + lane, 0)
    for s in (1, 2, 4, 8, 16, 32, 64):
        run = jnp.maximum(run, jnp.where(lane >= s, pltpu.roll(run, s, 1), 0))
    last = jnp.broadcast_to(jnp.max(run, axis=1, keepdims=True), doc.shape)
    carry = jnp.where(row >= 1, pltpu.roll(last, 1, 0), 0)
    for s in (1, 2, 4, 8, 16, 32, 64):
        carry = jnp.maximum(carry, jnp.where(row >= s, pltpu.roll(carry, s, 0), 0))
    start[...] = jnp.maximum(run, carry)

    for n in range(2):
        for j in range(NJ):
            arrived(kv_dst(n, j), a_rs.at[n, j])
    onward = (
        (2, dev(me, other, c), 0),
        (1, dev(me, y, hop(1)), (c + 1) // NCTX),
        (1, dev(me, other, hop(1)), (c + 1) // NCTX),
        (0, dev(me, y, hop(2)), (c + 2) // NCTX),
        (0, dev(me, other, hop(2)), (c + 2) // NCTX),
    )

    def onward_copy(n, a):
        piece, to, ahead = onward[n]
        at = (a + ahead) % SLOTS
        return remote(kv.at[:, a, 2, :, y], kv.at[:, at, piece, :, y], f_ss.at[a, n], f_rs.at[at, n], to)

    def onward_slot(a, _):
        for n in range(5):
            onward_copy(n, a).start()
        return _

    lax.fori_loop(0, SLOTS, onward_slot, 0)

    def send_rest(a, _):
        send_q(a)
        return _

    lax.fori_loop(1, SLOTS, send_rest, 0)

    key_at = lax.broadcasted_iota(jnp.int32, (NKEY, HD), 0)
    lane8 = lax.broadcasted_iota(jnp.int32, (8, HD), 1)
    row_in = lane8 % GRP

    def dq_dst(a, j):
        return dq_ref.at[a, 0, :, pl.ds(pl.multiple_of(j * QW, QW), QW)]

    def chunk(a, i):
        xs = (x + i + (i // 2) * (1 - 2 * (i % 2))) % NX
        for nc in range(2):
            for n, to in enumerate((qr, gr)):
                arrived(to.at[a, 2 * xs + nc], q_rs.at[n, a, 2 * xs + nc])
        off = 2 * xs + y
        for h in range(HPG):
            at = pl.ds(h * HD, HD)
            qc[pl.ds(h * GRP, GRP), :] = qr[a, pl.ds(2 * xs, 2), :, at].reshape(GRP, HD)
            gc[pl.ds(h * GRP, GRP), :] = gr[a, pl.ds(2 * xs, 2), :, at].reshape(GRP, HD)
        for t in range(17):
            at = off + t
            kc[pl.ds(t * GRP, GRP), :] = kv[0, a, at // 8, (at % 8) // 2, at % 2]
            vc[pl.ds(t * GRP, GRP), :] = kv[1, a, at // 8, (at % 8) // 2, at % 2]
        first = (a * NCTX + c) * 256 + off * GRP
        line = jnp.broadcast_to(start[pl.ds((a * NCTX + c) * 2 + off // 4, 1), :], (8, HD))
        line = pltpu.roll(line, (HD - GRP * (off % 4)) % HD, 1)
        line = jnp.where(lane8 < GRP, line, 0)
        line = line + pltpu.roll(line, GRP, 1)
        line = line + pltpu.roll(line, 2 * GRP, 1)
        low = jnp.maximum(line - (first - 512), row_in + 1)[:1]
        high = (row_in + 512)[:1]
        bias[...] = jnp.where((key_at >= low) & (key_at <= high), 0.0, -1e30)
        nt = (((1,), (1,)), ((), ()))
        scores = lax.dot_general(kc[...], qc[...], nt, preferred_element_type=jnp.float32)
        dweights = lax.dot_general(vc[...], gc[...], nt, preferred_element_type=jnp.float32)
        both = jnp.concatenate([bias[...]] * (STACK // HD), axis=1)
        scaled = scores * (FACTOR * LOG2E) + both
        top = jnp.max(scaled, axis=0, keepdims=True)
        exponent = jnp.exp2(scaled - top)
        total = jnp.sum(exponent, axis=0, keepdims=True)
        cross = jnp.sum(exponent * dweights, axis=0, keepdims=True)
        inverse = 1.0 / total
        weights = exponent * inverse
        dscores = (weights * (dweights - cross * inverse)).astype(jnp.bfloat16)
        weights = weights.astype(jnp.bfloat16)
        nn = (((1,), (0,)), ((), ()))
        dv = lax.dot_general(weights, gc[...], nn, preferred_element_type=jnp.float32)
        dk = lax.dot_general(dscores, qc[...], nn, preferred_element_type=jnp.float32)
        tn = (((0,), (0,)), ((), ()))
        dq = lax.dot_general(dscores, kc[...], tn, preferred_element_type=jnp.float32)
        acc[0, pl.ds(off, 17)] += dk.reshape(17, GRP, HD)
        acc[1, pl.ds(off, 17)] += dv.reshape(17, GRP, HD)
        dq = (dq * FACTOR).astype(jnp.bfloat16)
        for h in range(HPG):
            dqs[a, pl.ds(2 * xs, 2), :, pl.ds(h * HD, HD)] = dq[h * GRP : (h + 1) * GRP].reshape(2, ROWS, HD)
        for nc in range(2):
            j = 2 * xs + nc

            @pl.when(j == me)
            def _():
                pltpu.make_async_copy(dqs.at[a, j], dq_dst(a, me), dq_rs.at[a, me]).start()

            @pl.when(j != me)
            def _():
                remote(dqs.at[a, j], dq_dst(a, me), dq_ss.at[a, j], dq_rs.at[a, me], dev(j, y, c)).start()

    near, far = 1 - (c + 15) // NCTX, 1 - (c + 14) // NCTX
    back = (
        (2, other, dev(me, other, c), 0),
        (1, y, dev(me, y, hop(-1)), near),
        (1, other, dev(me, other, hop(-1)), near),
        (0, y, dev(me, y, hop(-2)), far),
        (0, other, dev(me, other, hop(-2)), far),
    )

    def back_copy(n, a):
        piece, half, to, behind = back[n]
        at = (a + SLOTS - behind) % SLOTS
        return remote(dks.at[a, :, piece, :, half], rx.at[at, n], dk_ss.at[a, n], dk_rs.at[at, n], to)

    def slot(a, _):
        for n in range(5):
            arrived(rx.at[a, n], f_rs.at[a, n])
        acc[...] = jnp.zeros_like(acc)

        def one(i, _):
            chunk(a, i)
            return _

        lax.fori_loop(0, NX, one, 0)
        dks[a, 0] = (acc[0] * FACTOR).astype(jnp.bfloat16).reshape(3, NX, 2, GRP, HD)
        dks[a, 1] = acc[1].astype(jnp.bfloat16).reshape(3, NX, 2, GRP, HD)
        for xx in range(NX):
            dko[a, 0, xx] = acc[0, 16 + 2 * xx + y] * FACTOR
            dko[a, 1, xx] = acc[1, 16 + 2 * xx + y]
        for n in range(5):
            back_copy(n, a).start()
        return _

    lax.fori_loop(0, SLOTS, slot, 0)

    def reduce(a, _):
        for n in range(5):
            arrived(rx.at[a, n], dk_rs.at[a, n])
        total = dko[a]
        for n in range(5):
            total = total + rx[a, n].astype(jnp.float32)
        home[:, a] = total.astype(jnp.bfloat16)
        return _

    lax.fori_loop(0, SLOTS, reduce, 0)

    def home_src(n, j):
        return home.at[n, :, j // 2, pl.ds(pl.multiple_of((j % 2) * ROWS, ROWS), ROWS)]

    def home_dst(n, j):
        return (dk_ref, dv_ref)[n].at[:, 0, :, pl.ds(pl.multiple_of(j * HD, HD), HD)]

    for n in range(2):
        pltpu.make_async_copy(home_src(n, me), home_dst(n, me), h_rs.at[n, me]).start()
        for p in PEERS:
            j = peer(*p)
            remote(home_src(n, j), home_dst(n, me), h_ss.at[n, j], h_rs.at[n, me], dev(j, y, c)).start()

    def drain(a, _):
        for j in range(NJ):
            arrived(dqs.at[a, j], dq_rs.at[a, j])
        for p in PEERS:
            j = peer(*p)
            for n, to in enumerate((qr, gr)):
                arrived(to.at[a, j], q_ss.at[n, a, j])
            arrived(dqs.at[a, j], dq_ss.at[a, j])
        for n in range(5):
            arrived(rx.at[a, n], f_ss.at[a, n])
            arrived(rx.at[a, n], dk_ss.at[a, n])
        return _

    lax.fori_loop(0, SLOTS, drain, 0)
    for n in range(2):
        for p in PEERS:
            j = peer(*p)
            arrived(kv_dst(n, j), a_ss.at[n, j])
            arrived(kv_dst(n, j), h_ss.at[n, j])
        for j in range(NJ):
            arrived(kv_dst(n, j), h_rs.at[n, j])


def body(queries, key_vectors, value_vectors, grad_output, doc_ids):
    bf, f32, dma = jnp.bfloat16, jnp.float32, pltpu.SemaphoreType.DMA
    hbm = pl.BlockSpec(memory_space=pl.ANY)
    vmem = pltpu.VMEM
    like = jax.ShapeDtypeStruct
    return pl.pallas_call(
        kernel,
        out_shape=(
            like(queries.shape, bf),
            like(key_vectors.shape, bf),
            like(value_vectors.shape, bf),
        ),
        in_specs=[hbm] * 4 + [pl.BlockSpec(memory_space=vmem)],
        out_specs=(hbm,) * 3,
        scratch_shapes=[
            vmem((SLOTS, NJ, ROWS, QW), bf),
            vmem((SLOTS, NJ, ROWS, QW), bf),
            vmem((SLOTS, NJ, ROWS, QW), bf),
            vmem((2, SLOTS, 3, NX, 2, GRP, HD), bf),
            vmem((STACK, HD), bf),
            vmem((STACK, HD), bf),
            vmem((NKEY, HD), bf),
            vmem((NKEY, HD), bf),
            vmem((NKEY, HD), f32),
            vmem((HD, HD), jnp.int32),
            vmem((2, 24, GRP, HD), f32),
            vmem((SLOTS, 2, 3, NX, 2, GRP, HD), bf),
            vmem((SLOTS, 2, NX, GRP, HD), f32),
            vmem((SLOTS, 5, 2, NX, GRP, HD), bf),
            vmem((2, SLOTS, NX, GRP, HD), bf),
            dma((2, SLOTS, NJ)),
            dma((2, SLOTS, NJ)),
            dma((2, NJ)),
            dma((2, NJ)),
            dma((SLOTS, 5)),
            dma((SLOTS, 5)),
            dma((SLOTS, NJ)),
            dma((SLOTS, NJ)),
            dma((SLOTS, 5)),
            dma((SLOTS, 5)),
            dma((2, NJ)),
            dma((2, NJ)),
        ],
        compiler_params=pltpu.CompilerParams(
            collective_id=0, has_side_effects=True, vmem_limit_bytes=48 << 20
        ),
    )(queries, key_vectors, value_vectors, grad_output, doc_ids.reshape(HD, HD))


def solution(mesh):
    placed = P(None, "ctx", "head", None)
    return jax.shard_map(
        body,
        mesh=mesh,
        in_specs=(placed,) * 4 + (P(),),
        out_specs=(placed,) * 3,
        check_vma=False,
    )
```

```python
import functools
import math

import jax
import jax.numpy as jnp
from jax import lax
from jax.experimental import pallas as pl
from jax.experimental.pallas import tpu as pltpu
from jax.sharding import PartitionSpec as P

MESH = pl.DeviceIdType.MESH
HD = 128
NX = 4
NJ = 8
NCTX = 16
NZ = 8
SLOTS = 4
ROWS = 16
GRP = 32
HPG = 12
QW = HPG * HD
NKEY = 17 * GRP
STACK = HPG * GRP
LOG2E = 1.4426950408889634
FACTOR = 1.0 / math.sqrt(HD)
PEERS = tuple((dx, dc) for dx in (2, 1, 3, 0) for dc in (0, 1) if (dx, dc) != (0, 0))


def kernel(
    q_ref, k_ref, v_ref, g_ref, doc_ref, dq_ref, dk_ref, dv_ref,
    qr, gr, dqs, kv, qc, gc, kc, vc, bias, start, acc, dks, dko, rx, dsum, own, home,
    q_ss, q_rs, a_ss, a_rs, f_ss, f_rs, dq_ss, dq_rs, dk_ss, dk_rs, h_ss, h_rs,
):
    head = lax.axis_index("head")
    c = lax.axis_index("ctx")
    x, y, core = head // 4, (head // 2) % 2, head % 2
    me = x * 2 + core
    other = 1 - y

    def dev(nj, ny, nc):
        return dict(head=(nj // 2) * 4 + ny * 2 + nj % 2, ctx=nc)

    def hop(by):
        return (c + by + NCTX) % NCTX

    def peer(dx, dc):
        return ((x + dx) % NX) * 2 + (core + dc) % 2

    def remote(src, dst, ss, rs, to):
        return pltpu.make_async_remote_copy(
            src_ref=src, dst_ref=dst, send_sem=ss, recv_sem=rs, device_id=to, device_id_type=MESH
        )

    def arrived(ref, sem):
        pltpu.make_async_copy(ref, ref, sem).wait()

    barrier = pltpu.get_barrier_semaphore()
    partners = [dev(peer(*p), y, c) for p in PEERS] + [dev(me, other, c)]
    partners += [dev(me, ny, hop(b)) for b in (1, 2, -1, -2) for ny in (y, other)]
    for to in partners:
        pl.semaphore_signal(barrier, inc=1, device_id=to, device_id_type=MESH)
    pl.semaphore_wait(barrier, len(partners))

    def kv_src(ref, j):
        return ref.at[:, 0, :, pl.ds(pl.multiple_of(j * HD, HD), HD)]

    def kv_dst(n, j):
        return kv.at[n, :, 2, j // 2, y, pl.ds(pl.multiple_of((j % 2) * ROWS, ROWS), ROWS)]

    for p in PEERS:
        j = peer(*p)
        for n, ref in enumerate((k_ref, v_ref)):
            remote(kv_src(ref, j), kv_dst(n, me), a_ss.at[n, j], a_rs.at[n, me], dev(j, y, c)).start()
    for n, ref in enumerate((k_ref, v_ref)):
        pltpu.make_async_copy(kv_src(ref, me), kv_dst(n, me), a_rs.at[n, me]).start()

    def q_src(ref, a, j):
        return ref.at[a, 0, :, pl.ds(pl.multiple_of(j * QW, QW), QW)]

    def send_q(a):
        for p in PEERS:
            j = peer(*p)
            for n, (ref, to) in enumerate(((q_ref, qr), (g_ref, gr))):
                remote(q_src(ref, a, j), to.at[a, me], q_ss.at[n, a, j], q_rs.at[n, a, me], dev(j, y, c)).start()
        for n, (ref, to) in enumerate(((q_ref, qr), (g_ref, gr))):
            pltpu.make_async_copy(q_src(ref, a, me), to.at[a, me], q_rs.at[n, a, me]).start()

    send_q(0)

    doc = doc_ref[...]
    row = lax.broadcasted_iota(jnp.int32, doc.shape, 0)
    lane = lax.broadcasted_iota(jnp.int32, doc.shape, 1)
    before = pltpu.roll(doc, 1, 1)
    before = jnp.where(lane == 0, pltpu.roll(before, 1, 0), before)
    run = jnp.where(doc != before, row * HD + lane, 0)
    for s in (1, 2, 4, 8, 16, 32, 64):
        run = jnp.maximum(run, jnp.where(lane >= s, pltpu.roll(run, s, 1), 0))
    last = jnp.broadcast_to(jnp.max(run, axis=1, keepdims=True), doc.shape)
    carry = jnp.where(row >= 1, pltpu.roll(last, 1, 0), 0)
    for s in (1, 2, 4, 8, 16, 32, 64):
        carry = jnp.maximum(carry, jnp.where(row >= s, pltpu.roll(carry, s, 0), 0))
    start[...] = jnp.maximum(run, carry)

    for n in range(2):
        for j in range(NJ):
            arrived(kv_dst(n, j), a_rs.at[n, j])
    z = c % NZ
    over, step = dev(me, other, c), (c + 1) // NCTX
    after = dev(me, (y + (z + 1) // NZ) % 2, hop(1))
    halves = ((y + 1 - (z + NZ - 2) // NZ) % 2, (y + 1 - (z + NZ - 1) // NZ) % 2, y)

    def half(a, piece, of):
        return kv.at[:, a, piece, :, halves[of]]

    def own_out(a):
        at = (a + step) % SLOTS
        return (
            remote(half(a, 2, 2), half(a, 2, 2), f_ss.at[a, 0], f_rs.at[a, 0], over),
            remote(half(a, 2, 2), half(at, 1, 2), f_ss.at[a, 1], f_rs.at[at, 1], after),
        )

    def near_out(a):
        at = (a + step) % SLOTS
        return (
            remote(half(a, 1, 1), half(at, 0, 1), f_ss.at[a, 3], f_rs.at[at, 3], after),
            remote(half(a, 1, 1), half(a, 1, 1), f_ss.at[a, 2], f_rs.at[a, 2], over),
        )

    def far_out(a):
        return (remote(half(a, 0, 0), half(a, 0, 0), f_ss.at[a, 4], f_rs.at[a, 4], over),)

    def onward(copies, a, came=None):
        if came is not None:
            arrived(rx.at[a, 0], f_rs.at[a, came])
        for copy in copies(a):
            copy.start()

    def own_slot(a, _):
        onward(own_out, a)
        return _

    lax.fori_loop(0, SLOTS, own_slot, 0)

    def send_rest(a, _):
        send_q(a)
        return _

    lax.fori_loop(1, SLOTS, send_rest, 0)

    def near_slot(a, _):
        onward(near_out, a, 1)
        return _

    lax.fori_loop(0, SLOTS, near_slot, 0)
    onward(far_out, 0, 3)

    key_at = lax.broadcasted_iota(jnp.int32, (NKEY, HD), 0)
    lane8 = lax.broadcasted_iota(jnp.int32, (8, HD), 1)
    row_in = lane8 % GRP

    def dq_dst(a, j):
        return dq_ref.at[a, 0, :, pl.ds(pl.multiple_of(j * QW, QW), QW)]

    def chunk(a, i):
        xs = (x + 2 * (i % 2) + i // 2) % NX
        for nc in range(2):
            for n, to in enumerate((qr, gr)):
                arrived(to.at[a, 2 * xs + nc], q_rs.at[n, a, 2 * xs + nc])
        off = 2 * xs + y
        for h in range(HPG):
            at = pl.ds(h * HD, HD)
            qc[pl.ds(h * GRP, GRP), :] = qr[a, pl.ds(2 * xs, 2), :, at].reshape(GRP, HD)
            gc[pl.ds(h * GRP, GRP), :] = gr[a, pl.ds(2 * xs, 2), :, at].reshape(GRP, HD)
        for t in range(17):
            at = off + t
            kc[pl.ds(t * GRP, GRP), :] = kv[0, a, at // 8, (at % 8) // 2, at % 2]
            vc[pl.ds(t * GRP, GRP), :] = kv[1, a, at // 8, (at % 8) // 2, at % 2]
        first = (a * NCTX + c) * 256 + off * GRP
        line = jnp.broadcast_to(start[pl.ds((a * NCTX + c) * 2 + off // 4, 1), :], (8, HD))
        line = pltpu.roll(line, (HD - GRP * (off % 4)) % HD, 1)
        line = jnp.where(lane8 < GRP, line, 0)
        line = line + pltpu.roll(line, GRP, 1)
        line = line + pltpu.roll(line, 2 * GRP, 1)
        low = jnp.maximum(line - (first - 512), row_in + 1)[:1]
        high = (row_in + 512)[:1]
        bias[...] = jnp.where((key_at >= low) & (key_at <= high), 0.0, -1e30)
        nt = (((1,), (1,)), ((), ()))
        scores = lax.dot_general(kc[...], qc[...], nt, preferred_element_type=jnp.float32)
        dweights = lax.dot_general(vc[...], gc[...], nt, preferred_element_type=jnp.float32)
        both = jnp.concatenate([bias[...]] * (STACK // HD), axis=1)
        scaled = scores * (FACTOR * LOG2E) + both
        top = jnp.max(scaled, axis=0, keepdims=True)
        exponent = jnp.exp2(scaled - top)
        total = jnp.sum(exponent, axis=0, keepdims=True)
        cross = jnp.sum(exponent * dweights, axis=0, keepdims=True)
        inverse = 1.0 / total
        weights = exponent * inverse
        dscores = (weights * (dweights - cross * inverse)).astype(jnp.bfloat16)
        weights = weights.astype(jnp.bfloat16)
        nn = (((1,), (0,)), ((), ()))
        dv = lax.dot_general(weights, gc[...], nn, preferred_element_type=jnp.float32)
        dk = lax.dot_general(dscores, qc[...], nn, preferred_element_type=jnp.float32)
        tn = (((0,), (0,)), ((), ()))
        dq = lax.dot_general(dscores, kc[...], tn, preferred_element_type=jnp.float32)
        acc[0, pl.ds(off, 17)] += dk.reshape(17, GRP, HD)
        acc[1, pl.ds(off, 17)] += dv.reshape(17, GRP, HD)
        dq = (dq * FACTOR).astype(jnp.bfloat16)
        for h in range(HPG):
            dqs[a, pl.ds(2 * xs, 2), :, pl.ds(h * HD, HD)] = dq[h * GRP : (h + 1) * GRP].reshape(2, ROWS, HD)
        for nc in range(2):
            j = 2 * xs + nc

            @pl.when(j == me)
            def _():
                pltpu.make_async_copy(dqs.at[a, j], dq_dst(a, me), dq_rs.at[a, me]).start()

            @pl.when(j != me)
            def _():
                remote(dqs.at[a, j], dq_dst(a, me), dq_ss.at[a, j], dq_rs.at[a, me], dev(j, y, c)).start()

    def swap_copy(a, piece):
        return remote(dks.at[a, piece], rx.at[a, piece], dk_ss.at[a, piece], dk_rs.at[a, piece], over)

    def swap(a):
        for piece in range(3):
            for n, scale in enumerate((FACTOR, 1.0)):
                for xx in range(NX):
                    at = piece * 8 + 2 * xx
                    dko[a, piece, n, xx] = acc[n, at + halves[piece]] * scale
                    dks[a, piece, n, xx] = (acc[n, at + 1 - halves[piece]] * scale).astype(jnp.bfloat16)
            swap_copy(a, piece).start()

    def owner_copy(a, piece):
        hops = 2 - piece
        at = (a + SLOTS - 1 + (c + NCTX - hops) // NCTX) % SLOTS
        to = dev(me, halves[piece], hop(-hops))
        return remote(dsum.at[a, piece], own.at[at, piece], dk_ss.at[a, 3 + piece], dk_rs.at[at, 3 + piece], to)

    def pass_back(a):
        for piece in range(2):
            arrived(rx.at[a, piece], dk_rs.at[a, piece])
            dsum[a, piece] = (dko[a, piece] + rx[a, piece].astype(jnp.float32)).astype(jnp.bfloat16)
            owner_copy(a, piece).start()

    def slot(a, carry):
        @pl.when(a < SLOTS - 1)
        def _():
            onward(far_out, a + 1, 3)

        for n in (0, 2, 4):
            arrived(rx.at[a, 0], f_rs.at[a, n])
        acc[...] = jnp.zeros_like(acc)

        def one(i, carry):
            chunk(a, i)

            @pl.when((i == 1) & (a > 0))
            def _():
                pass_back(a - 1)

            return carry

        lax.fori_loop(0, NX, one, 0)
        swap(a)
        return carry

    lax.fori_loop(0, SLOTS, slot, 0)

    pass_back(SLOTS - 1)

    def reduce(a, _):
        for n in (2, 3, 4):
            arrived(rx.at[a, 0], dk_rs.at[a, n])
        total = dko[a, 2] + rx[a, 2].astype(jnp.float32)
        for n in range(2):
            total = total + own[a, n].astype(jnp.float32)
        home[:, a] = total.astype(jnp.bfloat16)
        return _

    def home_src(n, j, at):
        return home.at[n, at, j // 2, pl.ds(pl.multiple_of((j % 2) * ROWS, ROWS), ROWS)]

    def home_dst(n, j, at):
        return (dk_ref, dv_ref)[n].at[at, 0, :, pl.ds(pl.multiple_of(j * HD, HD), HD)]

    for part, (low, many) in enumerate(((0, SLOTS - 1), (SLOTS - 1, 1))):
        lax.fori_loop(low, low + many, reduce, 0)
        at = pl.ds(low, many)
        for n in range(2):
            pltpu.make_async_copy(home_src(n, me, at), home_dst(n, me, at), h_rs.at[part, n, me]).start()
            for p in PEERS:
                j = peer(*p)
                remote(
                    home_src(n, j, at), home_dst(n, me, at), h_ss.at[part, n, j], h_rs.at[part, n, me], dev(j, y, c)
                ).start()

    def drain(a, _):
        for j in range(NJ):
            arrived(dqs.at[a, j], dq_rs.at[a, j])
        for p in PEERS:
            j = peer(*p)
            for n, to in enumerate((qr, gr)):
                arrived(to.at[a, j], q_ss.at[n, a, j])
            arrived(dqs.at[a, j], dq_ss.at[a, j])
        for n in range(5):
            arrived(rx.at[a, 0], f_ss.at[a, n])
            arrived(rx.at[a, 0], dk_ss.at[a, n])
        return _

    lax.fori_loop(0, SLOTS, drain, 0)
    for n in range(2):
        for p in PEERS:
            j = peer(*p)
            arrived(kv_dst(n, j), a_ss.at[n, j])
        for part, at in enumerate((pl.ds(0, SLOTS - 1), pl.ds(SLOTS - 1, 1))):
            for p in PEERS:
                arrived(home_src(n, 0, at), h_ss.at[part, n, peer(*p)])
            for j in range(NJ):
                arrived(home_src(n, 0, at), h_rs.at[part, n, j])


def body(queries, key_vectors, value_vectors, grad_output, doc_ids):
    bf, f32, dma = jnp.bfloat16, jnp.float32, pltpu.SemaphoreType.DMA
    hbm = pl.BlockSpec(memory_space=pltpu.HBM)
    vmem = pltpu.VMEM
    like = jax.ShapeDtypeStruct
    return pl.pallas_call(
        kernel,
        out_shape=(
            like(queries.shape, bf),
            like(key_vectors.shape, bf),
            like(value_vectors.shape, bf),
        ),
        in_specs=[hbm] * 4 + [pl.BlockSpec(memory_space=vmem)],
        out_specs=(hbm,) * 3,
        scratch_shapes=[
            vmem((SLOTS, NJ, ROWS, QW), bf),
            vmem((SLOTS, NJ, ROWS, QW), bf),
            vmem((SLOTS, NJ, ROWS, QW), bf),
            vmem((2, SLOTS, 3, NX, 2, GRP, HD), bf),
            vmem((STACK, HD), bf),
            vmem((STACK, HD), bf),
            vmem((NKEY, HD), bf),
            vmem((NKEY, HD), bf),
            vmem((NKEY, HD), f32),
            vmem((HD, HD), jnp.int32),
            vmem((2, 24, GRP, HD), f32),
            vmem((SLOTS, 3, 2, NX, GRP, HD), bf),
            vmem((SLOTS, 3, 2, NX, GRP, HD), f32),
            vmem((SLOTS, 3, 2, NX, GRP, HD), bf),
            vmem((SLOTS, 2, 2, NX, GRP, HD), bf),
            vmem((SLOTS, 2, 2, NX, GRP, HD), bf),
            vmem((2, SLOTS, NX, GRP, HD), bf),
            dma((2, SLOTS, NJ)),
            dma((2, SLOTS, NJ)),
            dma((2, NJ)),
            dma((2, NJ)),
            dma((SLOTS, 5)),
            dma((SLOTS, 5)),
            dma((SLOTS, NJ)),
            dma((SLOTS, NJ)),
            dma((SLOTS, 5)),
            dma((SLOTS, 5)),
            dma((2, 2, NJ)),
            dma((2, 2, NJ)),
        ],
        compiler_params=pltpu.CompilerParams(
            collective_id=0, has_side_effects=True, vmem_limit_bytes=62 << 20
        ),
    )(queries, key_vectors, value_vectors, grad_output, doc_ids.reshape(HD, HD))


def solution(mesh):
    placed = P(None, "ctx", "head", None)
    return jax.shard_map(
        body,
        mesh=mesh,
        in_specs=(placed,) * 4 + (P(),),
        out_specs=(placed,) * 3,
        check_vma=False,
    )
```

```python
import functools
import math

import jax
import jax.numpy as jnp
from jax import lax
from jax.experimental import pallas as pl
from jax.experimental.pallas import tpu as pltpu
from jax.sharding import PartitionSpec as P

MESH = pl.DeviceIdType.MESH
HD = 128
NX = 4
NJ = 8
NCTX = 16
NZ = 8
SLOTS = 4
ROWS = 16
GRP = 32
HPG = 12
QW = HPG * HD
NKEY = 17 * GRP
STACK = HPG * GRP
LOG2E = 1.4426950408889634
FACTOR = 1.0 / math.sqrt(HD)
PEERS = tuple((dx, dc) for dx in (2, 1, 3, 0) for dc in (0, 1) if (dx, dc) != (0, 0))


def kernel(
    q_ref, k_ref, v_ref, g_ref, doc_ref, dq_ref, dk_ref, dv_ref,
    qr, gr, dqs, kv, qc, gc, kc, vc, bias, start, acc, dks, dko, rx, dsum, own, home,
    q_ss, q_rs, a_ss, a_rs, f_ss, f_rs, dq_ss, dq_rs, dk_ss, dk_rs, h_ss, h_rs, met,
):
    head = lax.axis_index("head")
    c = lax.axis_index("ctx")
    x, y, core = head // 4, (head // 2) % 2, head % 2
    me = x * 2 + core
    other = 1 - y

    def dev(nj, ny, nc):
        return dict(head=(nj // 2) * 4 + ny * 2 + nj % 2, ctx=nc)

    def hop(by):
        return (c + by + NCTX) % NCTX

    def peer(dx, dc):
        return ((x + dx) % NX) * 2 + (core + dc) % 2

    def remote(src, dst, ss, rs, to):
        return pltpu.make_async_remote_copy(
            src_ref=src, dst_ref=dst, send_sem=ss, recv_sem=rs, device_id=to, device_id_type=MESH
        )

    def arrived(ref, sem):
        pltpu.make_async_copy(ref, ref, sem).wait()

    z = c % NZ
    barrier = pltpu.get_barrier_semaphore()
    over = dev(me, other, c)
    after = dev(me, (y + (z + 1) // NZ) % 2, hop(1))

    def announce(to):
        pl.semaphore_signal(barrier, inc=1, device_id=to, device_id_type=MESH)

    for dx in range(1, NX):
        announce(dev(((x + dx) % NX) * 2, y, c))

    @pl.when(core == 1)
    def _():
        announce(dev(2 * x, y, c))

    y_before, y_two = (y + 1 - (z + NZ - 1) // NZ) % 2, (y + (z + 2) // NZ) % 2
    for ny, by in ((other, 0), ((y + (z + 1) // NZ) % 2, 1), (y_before, -1), (y_two, 2)):
        announce(dev(2 * x + 1, ny, hop(by)))

    def tell(sem):
        pl.semaphore_signal(sem, inc=1, device_id=dev(2 * x + 1 - core, y, c), device_id_type=MESH)

    @pl.when(core == 0)
    def _():
        pl.semaphore_wait(barrier, NJ - 1)
        tell(met)

    @pl.when(core == 1)
    def _():
        pl.semaphore_wait(met, 1)

    def kv_src(ref, j):
        return ref.at[:, 0, :, pl.ds(pl.multiple_of(j * HD, HD), HD)]

    def kv_dst(n, j):
        return kv.at[n, :, 2, j // 2, y, pl.ds(pl.multiple_of((j % 2) * ROWS, ROWS), ROWS)]

    for p in PEERS:
        j = peer(*p)
        for n, ref in enumerate((k_ref, v_ref)):
            remote(kv_src(ref, j), kv_dst(n, me), a_ss.at[n, j], a_rs.at[n, me], dev(j, y, c)).start()
    for n, ref in enumerate((k_ref, v_ref)):
        pltpu.make_async_copy(kv_src(ref, me), kv_dst(n, me), a_rs.at[n, me]).start()

    def q_src(ref, a, j):
        return ref.at[a, 0, :, pl.ds(pl.multiple_of(j * QW, QW), QW)]

    def send_q(a):
        for p in PEERS:
            j = peer(*p)
            for n, (ref, to) in enumerate(((q_ref, qr), (g_ref, gr))):
                remote(q_src(ref, a, j), to.at[a, me], q_ss.at[n, a, j], q_rs.at[n, a, me], dev(j, y, c)).start()
        for n, (ref, to) in enumerate(((q_ref, qr), (g_ref, gr))):
            pltpu.make_async_copy(q_src(ref, a, me), to.at[a, me], q_rs.at[n, a, me]).start()

    send_q(0)

    def send_rest(a, _):
        send_q(a)
        return _

    lax.fori_loop(1, SLOTS, send_rest, 0)

    doc = doc_ref[...]
    row = lax.broadcasted_iota(jnp.int32, doc.shape, 0)
    lane = lax.broadcasted_iota(jnp.int32, doc.shape, 1)
    before = pltpu.roll(doc, 1, 1)
    before = jnp.where(lane == 0, pltpu.roll(before, 1, 0), before)
    run = jnp.where(doc != before, row * HD + lane, 0)
    for s in (1, 2, 4, 8, 16, 32, 64):
        run = jnp.maximum(run, jnp.where(lane >= s, pltpu.roll(run, s, 1), 0))
    last = jnp.broadcast_to(jnp.max(run, axis=1, keepdims=True), doc.shape)
    carry = jnp.where(row >= 1, pltpu.roll(last, 1, 0), 0)
    for s in (1, 2, 4, 8, 16, 32, 64):
        carry = jnp.maximum(carry, jnp.where(row >= s, pltpu.roll(carry, s, 0), 0))
    start[...] = jnp.maximum(run, carry)

    for n in range(2):
        for j in range(NJ):
            arrived(kv_dst(n, j), a_rs.at[n, j])
    step = (c + 1) // NCTX
    halves = ((y + 1 - (z + NZ - 2) // NZ) % 2, (y + 1 - (z + NZ - 1) // NZ) % 2, y)

    def half(a, piece, of):
        return kv.at[:, a, piece, :, halves[of]]

    for first, piece in ((0, 0), (0, 1), (1, 0)):

        @pl.when(c == first)
        def _(piece=piece):
            kv[:, 0, piece] = jnp.zeros((2, NX, 2, GRP, HD), jnp.bfloat16)

    def sends_near(a):
        return (c < NCTX - 1) | (a < SLOTS - 1)

    def has_near(a):
        return (c > 0) | (a > 0)

    def has_far(a):
        return (c > 1) | (a > 0)

    def own_over(a):
        return remote(half(a, 2, 2), half(a, 2, 2), f_ss.at[a, 0], f_rs.at[a, 0], over)

    def own_after(a):
        at = (a + step) % SLOTS
        return remote(half(a, 2, 2), half(at, 1, 2), f_ss.at[a, 1], f_rs.at[at, 1], after)

    def near_after(a):
        at = (a + step) % SLOTS
        return remote(half(a, 1, 1), half(at, 0, 1), f_ss.at[a, 3], f_rs.at[at, 3], after)

    def near_over(a):
        return remote(half(a, 1, 1), half(a, 1, 1), f_ss.at[a, 2], f_rs.at[a, 2], over)

    def far_over(a):
        return remote(half(a, 0, 0), half(a, 0, 0), f_ss.at[a, 4], f_rs.at[a, 4], over)

    def came(a, n):
        arrived(rx.at[a, 0], f_rs.at[a, n])

    @pl.when(core == 1)
    def _():
        pl.semaphore_wait(barrier, 8)
        tell(met)

    @pl.when(core == 0)
    def _():
        pl.semaphore_wait(met, 1)

    def own_slot(a, carry):
        @pl.when(sends_near(a))
        def _():
            own_after(a).start()

        own_over(a).start()
        return carry

    lax.fori_loop(0, SLOTS, own_slot, 0)

    def near_slot(a, carry):
        @pl.when(has_near(a))
        def _():
            came(a, 1)

            @pl.when(sends_near(a))
            def _():
                near_after(a).start()

            near_over(a).start()

        return carry

    lax.fori_loop(0, SLOTS, near_slot, 0)

    def far_slot(a):
        @pl.when((a < SLOTS) & has_far(a))
        def _():
            came(a, 3)
            far_over(a).start()

    far_slot(0)

    key_at = lax.broadcasted_iota(jnp.int32, (NKEY, HD), 0)
    lane8 = lax.broadcasted_iota(jnp.int32, (8, HD), 1)
    row_in = lane8 % GRP

    def dq_dst(a, j):
        return dq_ref.at[a, 0, :, pl.ds(pl.multiple_of(j * QW, QW), QW)]

    def chunk(a, i):
        xs = (x + 2 * (i % 2) + i // 2) % NX
        for nc in range(2):
            for n, to in enumerate((qr, gr)):
                arrived(to.at[a, 2 * xs + nc], q_rs.at[n, a, 2 * xs + nc])
        off = 2 * xs + y
        for h in range(HPG):
            at = pl.ds(h * HD, HD)
            qc[pl.ds(h * GRP, GRP), :] = qr[a, pl.ds(2 * xs, 2), :, at].reshape(GRP, HD)
            gc[pl.ds(h * GRP, GRP), :] = gr[a, pl.ds(2 * xs, 2), :, at].reshape(GRP, HD)
        for t in range(17):
            at = off + t
            kc[pl.ds(t * GRP, GRP), :] = kv[0, a, at // 8, (at % 8) // 2, at % 2]
            vc[pl.ds(t * GRP, GRP), :] = kv[1, a, at // 8, (at % 8) // 2, at % 2]
        first = (a * NCTX + c) * 256 + off * GRP
        line = jnp.broadcast_to(start[pl.ds((a * NCTX + c) * 2 + off // 4, 1), :], (8, HD))
        line = pltpu.roll(line, (HD - GRP * (off % 4)) % HD, 1)
        line = jnp.where(lane8 < GRP, line, 0)
        line = line + pltpu.roll(line, GRP, 1)
        line = line + pltpu.roll(line, 2 * GRP, 1)
        low = jnp.maximum(line - (first - 512), row_in + 1)[:1]
        high = (row_in + 512)[:1]
        bias[...] = jnp.where((key_at >= low) & (key_at <= high), 0.0, -1e30)
        nt = (((1,), (1,)), ((), ()))
        scores = lax.dot_general(kc[...], qc[...], nt, preferred_element_type=jnp.float32)
        dweights = lax.dot_general(vc[...], gc[...], nt, preferred_element_type=jnp.float32)
        both = jnp.concatenate([bias[...]] * (STACK // HD), axis=1)
        scaled = scores * (FACTOR * LOG2E) + both
        top = jnp.max(scaled, axis=0, keepdims=True)
        exponent = jnp.exp2(scaled - top)
        total = jnp.sum(exponent, axis=0, keepdims=True)
        cross = jnp.sum(exponent * dweights, axis=0, keepdims=True)
        inverse = 1.0 / total
        weights = exponent * inverse
        dscores = (weights * (dweights - cross * inverse)).astype(jnp.bfloat16)
        weights = weights.astype(jnp.bfloat16)
        nn = (((1,), (0,)), ((), ()))
        dv = lax.dot_general(weights, gc[...], nn, preferred_element_type=jnp.float32)
        dk = lax.dot_general(dscores, qc[...], nn, preferred_element_type=jnp.float32)
        tn = (((0,), (0,)), ((), ()))
        dq = lax.dot_general(dscores, kc[...], tn, preferred_element_type=jnp.float32)
        acc[0, pl.ds(off, 17)] += dk.reshape(17, GRP, HD)
        acc[1, pl.ds(off, 17)] += dv.reshape(17, GRP, HD)
        dq = (dq * FACTOR).astype(jnp.bfloat16)
        for h in range(HPG):
            dqs[a, pl.ds(2 * xs, 2), :, pl.ds(h * HD, HD)] = dq[h * GRP : (h + 1) * GRP].reshape(2, ROWS, HD)
        for nc in range(2):
            j = 2 * xs + nc

            @pl.when(j == me)
            def _():
                pltpu.make_async_copy(dqs.at[a, j], dq_dst(a, me), dq_rs.at[a, me]).start()

            @pl.when(j != me)
            def _():
                remote(dqs.at[a, j], dq_dst(a, me), dq_ss.at[a, j], dq_rs.at[a, me], dev(j, y, c)).start()

    def swap_copy(a, piece):
        return remote(dks.at[a, piece], rx.at[a, piece], dk_ss.at[a, piece], dk_rs.at[a, piece], over)

    def swap(a):
        for piece in range(3):
            for n, scale in enumerate((FACTOR, 1.0)):
                for xx in range(NX):
                    at = piece * 8 + 2 * xx
                    dko[a, piece, n, xx] = acc[n, at + halves[piece]] * scale
                    dks[a, piece, n, xx] = (acc[n, at + 1 - halves[piece]] * scale).astype(jnp.bfloat16)
            swap_copy(a, piece).start()

    def owner_copy(a, piece):
        hops = 2 - piece
        at = (a + SLOTS - 1 + (c + NCTX - hops) // NCTX) % SLOTS
        to = dev(me, halves[piece], hop(-hops))
        return remote(dsum.at[a, piece], own.at[at, piece], dk_ss.at[a, 3 + piece], dk_rs.at[at, 3 + piece], to)

    def pass_back(a):
        for piece in range(2):
            arrived(rx.at[a, piece], dk_rs.at[a, piece])
            dsum[a, piece] = (dko[a, piece] + rx[a, piece].astype(jnp.float32)).astype(jnp.bfloat16)
            owner_copy(a, piece).start()

    def slot(a, carry):
        far_slot(a + 1)
        came(a, 0)

        @pl.when(has_near(a))
        def _():
            came(a, 2)

        @pl.when(has_far(a))
        def _():
            came(a, 4)

        acc[...] = jnp.zeros_like(acc)

        def one(i, carry):
            chunk(a, i)

            @pl.when((i == 1) & (a > 0))
            def _():
                pass_back(a - 1)

            return carry

        lax.fori_loop(0, NX, one, 0)
        swap(a)
        return carry

    lax.fori_loop(0, SLOTS, slot, 0)

    pass_back(SLOTS - 1)

    def reduce(a, _):
        for n in (2, 3, 4):
            arrived(rx.at[a, 0], dk_rs.at[a, n])
        total = dko[a, 2] + rx[a, 2].astype(jnp.float32)
        for n in range(2):
            total = total + own[a, n].astype(jnp.float32)
        home[:, a] = total.astype(jnp.bfloat16)
        return _

    def home_src(n, j, at):
        return home.at[n, at, j // 2, pl.ds(pl.multiple_of((j % 2) * ROWS, ROWS), ROWS)]

    def home_dst(n, j, at):
        return (dk_ref, dv_ref)[n].at[at, 0, :, pl.ds(pl.multiple_of(j * HD, HD), HD)]

    for part, (low, many) in enumerate(((0, SLOTS - 1), (SLOTS - 1, 1))):
        lax.fori_loop(low, low + many, reduce, 0)
        at = pl.ds(low, many)
        for n in range(2):
            pltpu.make_async_copy(home_src(n, me, at), home_dst(n, me, at), h_rs.at[part, n, me]).start()
            for p in PEERS:
                j = peer(*p)
                remote(
                    home_src(n, j, at), home_dst(n, me, at), h_ss.at[part, n, j], h_rs.at[part, n, me], dev(j, y, c)
                ).start()

    def drain(a, _):
        for j in range(NJ):
            arrived(dqs.at[a, j], dq_rs.at[a, j])
        for p in PEERS:
            j = peer(*p)
            for n, to in enumerate((qr, gr)):
                arrived(to.at[a, j], q_ss.at[n, a, j])
            arrived(dqs.at[a, j], dq_ss.at[a, j])
        def sent(n):
            arrived(rx.at[a, 0], f_ss.at[a, n])

        sent(0)
        for n, when in ((1, sends_near(a)), (2, has_near(a)), (3, has_near(a) & sends_near(a)), (4, has_far(a))):
            pl.when(when)(functools.partial(sent, n))
        for n in range(5):
            arrived(rx.at[a, 0], dk_ss.at[a, n])
        return _

    lax.fori_loop(0, SLOTS, drain, 0)
    for n in range(2):
        for p in PEERS:
            j = peer(*p)
            arrived(kv_dst(n, j), a_ss.at[n, j])
        for part, at in enumerate((pl.ds(0, SLOTS - 1), pl.ds(SLOTS - 1, 1))):
            for p in PEERS:
                arrived(home_src(n, 0, at), h_ss.at[part, n, peer(*p)])
            for j in range(NJ):
                arrived(home_src(n, 0, at), h_rs.at[part, n, j])


def handed_on(dq, dk, dv, dq_out, dk_out, dv_out, dq_mid, dk_mid, dv_mid, sem):
    parts = [(dq, dq_mid, dq_out, a) for a in range(SLOTS)]
    parts += [(dk, dk_mid, dk_out, pl.ds(0, SLOTS)), (dv, dv_mid, dv_out, pl.ds(0, SLOTS))]
    ins = [pltpu.make_async_copy(r.at[at], m.at[at], sem.at[0, n]) for n, (r, m, _, at) in enumerate(parts)]
    outs = [pltpu.make_async_copy(m.at[at], o.at[at], sem.at[1, n]) for n, (_, m, o, at) in enumerate(parts)]
    for copy in ins:
        copy.start()
    for one, two in zip(ins, outs):
        one.wait()
        two.start()
    for copy in outs:
        copy.wait()


def body(queries, key_vectors, value_vectors, grad_output, doc_ids):
    bf, f32, dma = jnp.bfloat16, jnp.float32, pltpu.SemaphoreType.DMA
    hbm = pl.BlockSpec(memory_space=pltpu.HBM)
    vmem = pltpu.VMEM
    like = jax.ShapeDtypeStruct
    results = pl.pallas_call(
        kernel,
        out_shape=(
            like(queries.shape, bf),
            like(key_vectors.shape, bf),
            like(value_vectors.shape, bf),
        ),
        in_specs=[hbm] * 4 + [pl.BlockSpec(memory_space=vmem)],
        out_specs=(hbm,) * 3,
        scratch_shapes=[
            vmem((SLOTS, NJ, ROWS, QW), bf),
            vmem((SLOTS, NJ, ROWS, QW), bf),
            vmem((SLOTS, NJ, ROWS, QW), bf),
            vmem((2, SLOTS, 3, NX, 2, GRP, HD), bf),
            vmem((STACK, HD), bf),
            vmem((STACK, HD), bf),
            vmem((NKEY, HD), bf),
            vmem((NKEY, HD), bf),
            vmem((NKEY, HD), f32),
            vmem((HD, HD), jnp.int32),
            vmem((2, 24, GRP, HD), f32),
            vmem((SLOTS, 3, 2, NX, GRP, HD), bf),
            vmem((SLOTS, 3, 2, NX, GRP, HD), f32),
            vmem((SLOTS, 3, 2, NX, GRP, HD), bf),
            vmem((SLOTS, 2, 2, NX, GRP, HD), bf),
            vmem((SLOTS, 2, 2, NX, GRP, HD), bf),
            vmem((2, SLOTS, NX, GRP, HD), bf),
            dma((2, SLOTS, NJ)),
            dma((2, SLOTS, NJ)),
            dma((2, NJ)),
            dma((2, NJ)),
            dma((SLOTS, 5)),
            dma((SLOTS, 5)),
            dma((SLOTS, NJ)),
            dma((SLOTS, NJ)),
            dma((SLOTS, 5)),
            dma((SLOTS, 5)),
            dma((2, 2, NJ)),
            dma((2, 2, NJ)),
            pltpu.SemaphoreType.REGULAR,
        ],
        compiler_params=pltpu.CompilerParams(
            collective_id=0, has_side_effects=True, vmem_limit_bytes=62 << 20
        ),
    )(queries, key_vectors, value_vectors, grad_output, doc_ids.reshape(HD, HD))
    return pl.pallas_call(
        handed_on,
        out_shape=tuple(like(r.shape, bf) for r in results),
        in_specs=[hbm] * 3,
        out_specs=(hbm,) * 3,
        scratch_shapes=[vmem(r.shape, bf) for r in results] + [dma((2, 6))],
    )(*results)


def solution(mesh):
    placed = P(None, "ctx", "head", None)
    return jax.shard_map(
        body,
        mesh=mesh,
        in_specs=(placed,) * 4 + (P(),),
        out_specs=(placed,) * 3,
        check_vma=False,
    )
```

```python
import functools
import math

import jax
import jax.numpy as jnp
from jax import lax
from jax.experimental import pallas as pl
from jax.experimental.pallas import tpu as pltpu
from jax.sharding import PartitionSpec as P

MESH = pl.DeviceIdType.MESH
HD = 128
NX = 4
NJ = 8
NCTX = 16
NZ = 8
SLOTS = 4
ROWS = 16
GRP = 32
HPG = 12
QW = HPG * HD
NKEY = 17 * GRP
STACK = HPG * GRP
HOLD = 2
LOG2E = 1.4426950408889634
FACTOR = 1.0 / math.sqrt(HD)
PEERS = tuple((dx, dc) for dx in (2, 1, 3, 0) for dc in (0, 1) if (dx, dc) != (0, 0))


def kernel(
    q_ref, k_ref, v_ref, g_ref, doc_ref, dq_ref, dk_ref, dv_ref,
    qr, gr, dqs, kv, qc, gc, kc, vc, bias, start, acc, dks, dko, rx, dsum, own, home,
    q_ss, q_rs, a_ss, a_rs, f_ss, f_rs, dq_ss, dq_rs, dk_ss, dk_rs, h_ss, h_rs, met,
):
    head = lax.axis_index("head")
    c = lax.axis_index("ctx")
    x, y, core = head // 4, (head // 2) % 2, head % 2
    me = x * 2 + core
    other = 1 - y

    def dev(nj, ny, nc):
        return dict(head=(nj // 2) * 4 + ny * 2 + nj % 2, ctx=nc)

    def hop(by):
        return (c + by + NCTX) % NCTX

    def peer(dx, dc):
        return ((x + dx) % NX) * 2 + (core + dc) % 2

    def remote(src, dst, ss, rs, to):
        return pltpu.make_async_remote_copy(
            src_ref=src, dst_ref=dst, send_sem=ss, recv_sem=rs, device_id=to, device_id_type=MESH
        )

    def arrived(ref, sem):
        pltpu.make_async_copy(ref, ref, sem).wait()

    z = c % NZ
    barrier = pltpu.get_barrier_semaphore()
    over = dev(me, other, c)
    after = dev(me, (y + (z + 1) // NZ) % 2, hop(1))

    def announce(to):
        pl.semaphore_signal(barrier, inc=1, device_id=to, device_id_type=MESH)

    for dx in range(1, NX):
        announce(dev(((x + dx) % NX) * 2, y, c))

    @pl.when(core == 1)
    def _():
        announce(dev(2 * x, y, c))

    y_before, y_two = (y + 1 - (z + NZ - 1) // NZ) % 2, (y + (z + 2) // NZ) % 2
    for ny, by in ((other, 0), ((y + (z + 1) // NZ) % 2, 1), (y_before, -1), (y_two, 2)):
        announce(dev(2 * x + 1, ny, hop(by)))

    def tell(sem):
        pl.semaphore_signal(sem, inc=1, device_id=dev(2 * x + 1 - core, y, c), device_id_type=MESH)

    @pl.when(core == 0)
    def _():
        pl.semaphore_wait(barrier, NJ - 1)
        tell(met)

    @pl.when(core == 1)
    def _():
        pl.semaphore_wait(met, 1)

    def kv_src(ref, j):
        return ref.at[:, 0, :, pl.ds(pl.multiple_of(j * HD, HD), HD)]

    def kv_dst(n, j):
        return kv.at[n, :, 2, j // 2, y, pl.ds(pl.multiple_of((j % 2) * ROWS, ROWS), ROWS)]

    for p in PEERS:
        j = peer(*p)
        for n, ref in enumerate((k_ref, v_ref)):
            remote(kv_src(ref, j), kv_dst(n, me), a_ss.at[n], a_rs.at[n], dev(j, y, c)).start()
    for n, ref in enumerate((k_ref, v_ref)):
        pltpu.make_async_copy(kv_src(ref, me), kv_dst(n, me), a_rs.at[n]).start()

    def q_src(ref, a, j):
        return ref.at[a, 0, :, pl.ds(pl.multiple_of(j * QW, QW), QW)]

    def send_q(a):
        for p in PEERS:
            j = peer(*p)
            for n, (ref, to) in enumerate(((q_ref, qr), (g_ref, gr))):
                remote(q_src(ref, a, j), to.at[a, me], q_ss.at[n], q_rs.at[n, a, me], dev(j, y, c)).start()
        for n, (ref, to) in enumerate(((q_ref, qr), (g_ref, gr))):
            pltpu.make_async_copy(q_src(ref, a, me), to.at[a, me], q_rs.at[n, a, me]).start()

    send_q(0)

    def send_rest(a, _):
        send_q(a)
        return _

    lax.fori_loop(1, SLOTS, send_rest, 0)

    doc = doc_ref[...]
    row = lax.broadcasted_iota(jnp.int32, doc.shape, 0)
    lane = lax.broadcasted_iota(jnp.int32, doc.shape, 1)
    before = pltpu.roll(doc, 1, 1)
    before = jnp.where(lane == 0, pltpu.roll(before, 1, 0), before)
    run = jnp.where(doc != before, row * HD + lane, 0)
    for s in (1, 2, 4, 8, 16, 32, 64):
        run = jnp.maximum(run, jnp.where(lane >= s, pltpu.roll(run, s, 1), 0))
    last = jnp.broadcast_to(jnp.max(run, axis=1, keepdims=True), doc.shape)
    carry = jnp.where(row >= 1, pltpu.roll(last, 1, 0), 0)
    for s in (1, 2, 4, 8, 16, 32, 64):
        carry = jnp.maximum(carry, jnp.where(row >= s, pltpu.roll(carry, s, 0), 0))
    start[...] = jnp.maximum(run, carry)

    for n in range(2):
        arrived(kv.at[n, :, 2, :, y], a_rs.at[n])
    step = (c + 1) // NCTX
    halves = ((y + 1 - (z + NZ - 2) // NZ) % 2, (y + 1 - (z + NZ - 1) // NZ) % 2, y)

    def half(a, piece, of):
        return kv.at[:, a, piece, :, halves[of]]

    for first, piece in ((0, 0), (0, 1), (1, 0)):

        @pl.when(c == first)
        def _(piece=piece):
            kv[:, 0, piece] = jnp.zeros((2, NX, 2, GRP, HD), jnp.bfloat16)

    def sends_near(a):
        return (c < NCTX - 1) | (a < SLOTS - 1)

    def has_near(a):
        return (c > 0) | (a > 0)

    def has_far(a):
        return (c > 1) | (a > 0)

    def own_over(a):
        return remote(half(a, 2, 2), half(a, 2, 2), f_ss.at[a, 0], f_rs.at[a, 0], over)

    def own_after(a):
        at = (a + step) % SLOTS
        return remote(half(a, 2, 2), half(at, 1, 2), f_ss.at[a, 1], f_rs.at[at, 1], after)

    def near_after(a):
        at = (a + step) % SLOTS
        return remote(half(a, 1, 1), half(at, 0, 1), f_ss.at[a, 3], f_rs.at[at, 3], after)

    def near_over(a):
        return remote(half(a, 1, 1), half(a, 1, 1), f_ss.at[a, 2], f_rs.at[a, 2], over)

    def far_over(a):
        return remote(half(a, 0, 0), half(a, 0, 0), f_ss.at[a, 4], f_rs.at[a, 4], over)

    def came(a, n):
        arrived(rx.at[a, 0], f_rs.at[a, n])

    @pl.when(core == 1)
    def _():
        pl.semaphore_wait(barrier, 8)
        tell(met)

    @pl.when(core == 0)
    def _():
        pl.semaphore_wait(met, 1)

    def own_slot(a, carry):
        @pl.when(sends_near(a))
        def _():
            own_after(a).start()

        own_over(a).start()
        return carry

    lax.fori_loop(0, SLOTS, own_slot, 0)

    def near_slot(a, carry):
        @pl.when(has_near(a))
        def _():
            came(a, 1)

            @pl.when(sends_near(a))
            def _():
                near_after(a).start()

            near_over(a).start()

        return carry

    lax.fori_loop(0, SLOTS, near_slot, 0)

    def far_slot(a):
        @pl.when((a < SLOTS) & has_far(a))
        def _():
            came(a, 3)
            far_over(a).start()

    far_slot(0)

    key_at = lax.broadcasted_iota(jnp.int32, (NKEY, HD), 0)
    lane8 = lax.broadcasted_iota(jnp.int32, (8, HD), 1)
    row_in = lane8 % GRP

    def dq_dst(a, j):
        return dq_ref.at[a, 0, :, pl.ds(pl.multiple_of(j * QW, QW), QW)]

    def send_dq(a, xs):
        for nc in range(2):
            j = 2 * xs + nc

            @pl.when(j == me)
            def _(j=j):
                pltpu.make_async_copy(dqs.at[a, j], dq_dst(a, me), dq_rs.at[0]).start()

            @pl.when(j != me)
            def _(j=j):
                remote(dqs.at[a, j], dq_dst(a, me), dq_ss.at[0], dq_rs.at[0], dev(j, y, c)).start()

    def held_dq():
        def each(n, carry):
            send_dq(n // NX, (x + 2 * (n % 2) + (n % NX) // 2) % NX)
            return carry

        lax.fori_loop(0, HOLD * NX + 1, each, 0)

    def chunk(a, i):
        xs = (x + 2 * (i % 2) + i // 2) % NX
        for nc in range(2):
            for n, to in enumerate((qr, gr)):
                arrived(to.at[a, 2 * xs + nc], q_rs.at[n, a, 2 * xs + nc])
        pl.when((a == HOLD) & (i == 1))(held_dq)
        off = 2 * xs + y
        for h in range(HPG):
            at = pl.ds(h * HD, HD)
            qc[pl.ds(h * GRP, GRP), :] = qr[a, pl.ds(2 * xs, 2), :, at].reshape(GRP, HD)
            gc[pl.ds(h * GRP, GRP), :] = gr[a, pl.ds(2 * xs, 2), :, at].reshape(GRP, HD)
        for t in range(17):
            at = off + t
            kc[pl.ds(t * GRP, GRP), :] = kv[0, a, at // 8, (at % 8) // 2, at % 2]
            vc[pl.ds(t * GRP, GRP), :] = kv[1, a, at // 8, (at % 8) // 2, at % 2]
        first = (a * NCTX + c) * 256 + off * GRP
        line = jnp.broadcast_to(start[pl.ds((a * NCTX + c) * 2 + off // 4, 1), :], (8, HD))
        line = pltpu.roll(line, (HD - GRP * (off % 4)) % HD, 1)
        line = jnp.where(lane8 < GRP, line, 0)
        line = line + pltpu.roll(line, GRP, 1)
        line = line + pltpu.roll(line, 2 * GRP, 1)
        low = jnp.maximum(line - (first - 512), row_in + 1)[:1]
        high = (row_in + 512)[:1]
        bias[...] = jnp.where((key_at >= low) & (key_at <= high), 0.0, -1e30)
        nt = (((1,), (1,)), ((), ()))
        scores = lax.dot_general(kc[...], qc[...], nt, preferred_element_type=jnp.float32)
        dweights = lax.dot_general(vc[...], gc[...], nt, preferred_element_type=jnp.float32)
        both = jnp.concatenate([bias[...]] * (STACK // HD), axis=1)
        scaled = scores * (FACTOR * LOG2E) + both
        top = jnp.max(scaled, axis=0, keepdims=True)
        exponent = jnp.exp2(scaled - top)
        total = jnp.sum(exponent, axis=0, keepdims=True)
        cross = jnp.sum(exponent * dweights, axis=0, keepdims=True)
        inverse = 1.0 / total
        weights = exponent * inverse
        dscores = (weights * (dweights - cross * inverse)).astype(jnp.bfloat16)
        weights = weights.astype(jnp.bfloat16)
        nn = (((1,), (0,)), ((), ()))
        dv = lax.dot_general(weights, gc[...], nn, preferred_element_type=jnp.float32)
        dk = lax.dot_general(dscores, qc[...], nn, preferred_element_type=jnp.float32)
        tn = (((0,), (0,)), ((), ()))
        dq = lax.dot_general(dscores, kc[...], tn, preferred_element_type=jnp.float32)
        acc[0, pl.ds(off, 17)] += dk.reshape(17, GRP, HD)
        acc[1, pl.ds(off, 17)] += dv.reshape(17, GRP, HD)
        dq = (dq * FACTOR).astype(jnp.bfloat16)
        for h in range(HPG):
            dqs[a, pl.ds(2 * xs, 2), :, pl.ds(h * HD, HD)] = dq[h * GRP : (h + 1) * GRP].reshape(2, ROWS, HD)
        pl.when((a > HOLD) | ((a == HOLD) & (i > 0)))(functools.partial(send_dq, a, xs))

    def swap_copy(a, piece):
        return remote(dks.at[a, piece], rx.at[a, piece], dk_ss.at[a, piece], dk_rs.at[a, piece], over)

    def swap(a):
        for piece in range(3):
            for n, scale in enumerate((FACTOR, 1.0)):
                for xx in range(NX):
                    at = piece * 8 + 2 * xx
                    dko[a, piece, n, xx] = acc[n, at + halves[piece]] * scale
                    dks[a, piece, n, xx] = (acc[n, at + 1 - halves[piece]] * scale).astype(jnp.bfloat16)
            swap_copy(a, piece).start()

    def owner_copy(a, piece):
        hops = 2 - piece
        at = (a + SLOTS - 1 + (c + NCTX - hops) // NCTX) % SLOTS
        to = dev(me, halves[piece], hop(-hops))
        return remote(dsum.at[a, piece], own.at[at, piece], dk_ss.at[a, 3 + piece], dk_rs.at[at, 3 + piece], to)

    def pass_back(a):
        for piece in range(2):
            arrived(rx.at[a, piece], dk_rs.at[a, piece])
            dsum[a, piece] = (dko[a, piece] + rx[a, piece].astype(jnp.float32)).astype(jnp.bfloat16)
            owner_copy(a, piece).start()

    def slot(a, carry):
        far_slot(a + 1)
        came(a, 0)

        @pl.when(has_near(a))
        def _():
            came(a, 2)

        @pl.when(has_far(a))
        def _():
            came(a, 4)

        acc[...] = jnp.zeros_like(acc)

        def one(i, carry):
            chunk(a, i)

            @pl.when((i == 1) & (a > 0))
            def _():
                pass_back(a - 1)

            return carry

        lax.fori_loop(0, NX, one, 0)
        swap(a)
        return carry

    lax.fori_loop(0, SLOTS, slot, 0)

    for n, to in enumerate((qr, gr)):
        arrived(to.at[:, pl.ds(0, NJ - 1)], q_ss.at[n])
        arrived(kc.at[pl.ds(0, (NJ - 1) * SLOTS * ROWS)], a_ss.at[n])

    def sent_keys(a, carry):
        def sent(n):
            arrived(rx.at[a, 0], f_ss.at[a, n])

        sent(0)
        for n, when in ((1, sends_near(a)), (2, has_near(a)), (3, has_near(a) & sends_near(a)), (4, has_far(a))):
            pl.when(when)(functools.partial(sent, n))
        return carry

    lax.fori_loop(0, SLOTS, sent_keys, 0)

    def reduce(a, _):
        for n in (2, 3, 4):
            arrived(rx.at[a, 0], dk_rs.at[a, n])
        total = dko[a, 2] + rx[a, 2].astype(jnp.float32)
        for n in range(2):
            total = total + own[a, n].astype(jnp.float32)
        home[:, a] = total.astype(jnp.bfloat16)
        return _

    def home_src(n, j, at):
        return home.at[n, at, j // 2, pl.ds(pl.multiple_of((j % 2) * ROWS, ROWS), ROWS)]

    def home_dst(n, j, at):
        return (dk_ref, dv_ref)[n].at[at, 0, :, pl.ds(pl.multiple_of(j * HD, HD), HD)]

    def go_home(part):
        lax.fori_loop(2 * part, 2 * part + 2, reduce, 0)
        at = pl.ds(2 * part, 2)
        for p in PEERS:
            j = peer(*p)
            for n in range(2):
                remote(home_src(n, j, at), home_dst(n, me, at), h_ss.at[n], h_rs.at[n], dev(j, y, c)).start()
        for n in range(2):
            pltpu.make_async_copy(home_src(n, me, at), home_dst(n, me, at), h_rs.at[n]).start()

    go_home(0)
    pass_back(SLOTS - 1)
    go_home(1)

    def sent_grads(a, carry):
        for n in range(5):
            arrived(rx.at[a, 0], dk_ss.at[a, n])
        return carry

    lax.fori_loop(0, SLOTS, sent_grads, 0)
    arrived(dqs.at[:, pl.ds(0, NJ - 1)], dq_ss.at[0])
    arrived(dq_ref, dq_rs.at[0])
    for n, ref in enumerate((dk_ref, dv_ref)):
        arrived(kc.at[pl.ds(0, (NJ - 1) * SLOTS * ROWS)], h_ss.at[n])
        arrived(ref, h_rs.at[n])


def handed_on(dq, dk, dv, dq_out, dk_out, dv_out, dq_mid, dk_mid, dv_mid, sem):
    parts = [(dq, dq_mid, dq_out, a) for a in range(SLOTS)]
    parts += [(dk, dk_mid, dk_out, pl.ds(0, SLOTS)), (dv, dv_mid, dv_out, pl.ds(0, SLOTS))]
    ins = [pltpu.make_async_copy(r.at[at], m.at[at], sem.at[0, n]) for n, (r, m, _, at) in enumerate(parts)]
    outs = [pltpu.make_async_copy(m.at[at], o.at[at], sem.at[1, n]) for n, (_, m, o, at) in enumerate(parts)]
    for copy in ins:
        copy.start()
    for one, two in zip(ins, outs):
        one.wait()
        two.start()
    for copy in outs:
        copy.wait()


def body(queries, key_vectors, value_vectors, grad_output, doc_ids):
    bf, f32, dma = jnp.bfloat16, jnp.float32, pltpu.SemaphoreType.DMA
    hbm = pl.BlockSpec(memory_space=pltpu.HBM)
    vmem = pltpu.VMEM
    like = jax.ShapeDtypeStruct
    results = pl.pallas_call(
        kernel,
        out_shape=(
            like(queries.shape, bf),
            like(key_vectors.shape, bf),
            like(value_vectors.shape, bf),
        ),
        in_specs=[hbm] * 4 + [pl.BlockSpec(memory_space=vmem)],
        out_specs=(hbm,) * 3,
        scratch_shapes=[
            vmem((SLOTS, NJ, ROWS, QW), bf),
            vmem((SLOTS, NJ, ROWS, QW), bf),
            vmem((SLOTS, NJ, ROWS, QW), bf),
            vmem((2, SLOTS, 3, NX, 2, GRP, HD), bf),
            vmem((STACK, HD), bf),
            vmem((STACK, HD), bf),
            vmem((NKEY, HD), bf),
            vmem((NKEY, HD), bf),
            vmem((NKEY, HD), f32),
            vmem((HD, HD), jnp.int32),
            vmem((2, 24, GRP, HD), f32),
            vmem((SLOTS, 3, 2, NX, GRP, HD), bf),
            vmem((SLOTS, 3, 2, NX, GRP, HD), f32),
            vmem((SLOTS, 3, 2, NX, GRP, HD), bf),
            vmem((SLOTS, 2, 2, NX, GRP, HD), bf),
            vmem((SLOTS, 2, 2, NX, GRP, HD), bf),
            vmem((2, SLOTS, NX, GRP, HD), bf),
            dma((2,)),
            dma((2, SLOTS, NJ)),
            dma((2,)),
            dma((2,)),
            dma((SLOTS, 5)),
            dma((SLOTS, 5)),
            dma((1,)),
            dma((1,)),
            dma((SLOTS, 5)),
            dma((SLOTS, 5)),
            dma((2,)),
            dma((2,)),
            pltpu.SemaphoreType.REGULAR,
        ],
        compiler_params=pltpu.CompilerParams(
            collective_id=0, has_side_effects=True, vmem_limit_bytes=62 << 20
        ),
    )(queries, key_vectors, value_vectors, grad_output, doc_ids.reshape(HD, HD))
    return pl.pallas_call(
        handed_on,
        out_shape=tuple(like(r.shape, bf) for r in results),
        in_specs=[hbm] * 3,
        out_specs=(hbm,) * 3,
        scratch_shapes=[vmem(r.shape, bf) for r in results] + [dma((2, 6))],
    )(*results)


def solution(mesh):
    placed = P(None, "ctx", "head", None)
    return jax.shard_map(
        body,
        mesh=mesh,
        in_specs=(placed,) * 4 + (P(),),
        out_specs=(placed,) * 3,
        check_vma=False,
    )
```

```python
import functools
import math

import jax
import jax.numpy as jnp
from jax import lax
from jax.experimental import pallas as pl
from jax.experimental.pallas import tpu as pltpu
from jax.sharding import PartitionSpec as P

MESH = pl.DeviceIdType.MESH
HD = 128
NX = 4
NJ = 8
NCTX = 16
NZ = 8
SLOTS = 4
ROWS = 16
GRP = 32
HPG = 12
QW = HPG * HD
NKEY = 17 * GRP
STACK = HPG * GRP
HOLD = 3
LOG2E = 1.4426950408889634
FACTOR = 1.0 / math.sqrt(HD)
PEERS = tuple((dx, dc) for dx in (2, 1, 3, 0) for dc in (0, 1) if (dx, dc) != (0, 0))


def kernel(
    q_ref, k_ref, v_ref, g_ref, doc_ref, dq_ref, dk_ref, dv_ref,
    qr, gr, dqs, kv, qc, gc, kc, vc, bias, start, acc, dks, dko, rx, dsum, own, home,
    q_ss, q_rs, a_ss, a_rs, f_ss, f_rs, dq_ss, dq_rs, dk_ss, dk_rs, h_ss, h_rs, met,
):
    head = lax.axis_index("head")
    c = lax.axis_index("ctx")
    x, y, core = head // 4, (head // 2) % 2, head % 2
    me = x * 2 + core
    other = 1 - y

    def dev(nj, ny, nc):
        return dict(head=(nj // 2) * 4 + ny * 2 + nj % 2, ctx=nc)

    def hop(by):
        return (c + by + NCTX) % NCTX

    def peer(dx, dc):
        return ((x + dx) % NX) * 2 + (core + dc) % 2

    def remote(src, dst, ss, rs, to):
        return pltpu.make_async_remote_copy(
            src_ref=src, dst_ref=dst, send_sem=ss, recv_sem=rs, device_id=to, device_id_type=MESH
        )

    def arrived(ref, sem):
        pltpu.make_async_copy(ref, ref, sem).wait()

    z = c % NZ
    barrier = pltpu.get_barrier_semaphore()
    over = dev(me, other, c)
    after = dev(me, (y + (z + 1) // NZ) % 2, hop(1))

    def announce(to):
        pl.semaphore_signal(barrier, inc=1, device_id=to, device_id_type=MESH)

    for dx in range(1, NX):
        announce(dev(((x + dx) % NX) * 2, y, c))

    @pl.when(core == 1)
    def _():
        announce(dev(2 * x, y, c))

    y_before, y_two = (y + 1 - (z + NZ - 1) // NZ) % 2, (y + (z + 2) // NZ) % 2
    for ny, by in ((other, 0), ((y + (z + 1) // NZ) % 2, 1), (y_before, -1), (y_two, 2)):
        announce(dev(2 * x + 1, ny, hop(by)))

    def tell(sem):
        pl.semaphore_signal(sem, inc=1, device_id=dev(2 * x + 1 - core, y, c), device_id_type=MESH)

    @pl.when(core == 0)
    def _():
        pl.semaphore_wait(barrier, NJ - 1)
        tell(met)

    @pl.when(core == 1)
    def _():
        pl.semaphore_wait(met, 1)

    def kv_src(ref, j):
        return ref.at[:, 0, :, pl.ds(pl.multiple_of(j * HD, HD), HD)]

    def kv_dst(n, j):
        return kv.at[n, :, 2, j // 2, y, pl.ds(pl.multiple_of((j % 2) * ROWS, ROWS), ROWS)]

    for p in PEERS:
        j = peer(*p)
        for n, ref in enumerate((k_ref, v_ref)):
            remote(kv_src(ref, j), kv_dst(n, me), a_ss.at[n], a_rs.at[n], dev(j, y, c)).start()
    for n, ref in enumerate((k_ref, v_ref)):
        pltpu.make_async_copy(kv_src(ref, me), kv_dst(n, me), a_rs.at[n]).start()

    def q_src(ref, a, j):
        return ref.at[a, 0, :, pl.ds(pl.multiple_of(j * QW, QW), QW)]

    def send_q(a):
        for p in PEERS:
            j = peer(*p)
            for n, (ref, to) in enumerate(((q_ref, qr), (g_ref, gr))):
                remote(q_src(ref, a, j), to.at[a, me], q_ss.at[n], q_rs.at[n, a, me], dev(j, y, c)).start()
        for n, (ref, to) in enumerate(((q_ref, qr), (g_ref, gr))):
            pltpu.make_async_copy(q_src(ref, a, me), to.at[a, me], q_rs.at[n, a, me]).start()

    send_q(0)

    def send_rest(a, _):
        send_q(a)
        return _

    lax.fori_loop(1, SLOTS, send_rest, 0)

    doc = doc_ref[...]
    row = lax.broadcasted_iota(jnp.int32, doc.shape, 0)
    lane = lax.broadcasted_iota(jnp.int32, doc.shape, 1)
    before = pltpu.roll(doc, 1, 1)
    before = jnp.where(lane == 0, pltpu.roll(before, 1, 0), before)
    run = jnp.where(doc != before, row * HD + lane, 0)
    for s in (1, 2, 4, 8, 16, 32, 64):
        run = jnp.maximum(run, jnp.where(lane >= s, pltpu.roll(run, s, 1), 0))
    last = jnp.broadcast_to(jnp.max(run, axis=1, keepdims=True), doc.shape)
    carry = jnp.where(row >= 1, pltpu.roll(last, 1, 0), 0)
    for s in (1, 2, 4, 8, 16, 32, 64):
        carry = jnp.maximum(carry, jnp.where(row >= s, pltpu.roll(carry, s, 0), 0))
    start[...] = jnp.maximum(run, carry)

    for n in range(2):
        arrived(kv.at[n, :, 2, :, y], a_rs.at[n])
    step = (c + 1) // NCTX
    halves = ((y + 1 - (z + NZ - 2) // NZ) % 2, (y + 1 - (z + NZ - 1) // NZ) % 2, y)

    def half(a, piece, of):
        return kv.at[:, a, piece, :, halves[of]]

    for first, piece in ((0, 0), (0, 1), (1, 0)):

        @pl.when(c == first)
        def _(piece=piece):
            kv[:, 0, piece] = jnp.zeros((2, NX, 2, GRP, HD), jnp.bfloat16)

    def sends_near(a):
        return (c < NCTX - 1) | (a < SLOTS - 1)

    def has_near(a):
        return (c > 0) | (a > 0)

    def has_far(a):
        return (c > 1) | (a > 0)

    def own_over(a):
        return remote(half(a, 2, 2), half(a, 2, 2), f_ss.at[a, 0], f_rs.at[a, 0], over)

    def own_after(a):
        at = (a + step) % SLOTS
        return remote(half(a, 2, 2), half(at, 1, 2), f_ss.at[a, 1], f_rs.at[at, 1], after)

    def near_after(a):
        at = (a + step) % SLOTS
        return remote(half(a, 1, 1), half(at, 0, 1), f_ss.at[a, 3], f_rs.at[at, 3], after)

    def near_over(a):
        return remote(half(a, 1, 1), half(a, 1, 1), f_ss.at[a, 2], f_rs.at[a, 2], over)

    def far_over(a):
        return remote(half(a, 0, 0), half(a, 0, 0), f_ss.at[a, 4], f_rs.at[a, 4], over)

    def came(a, n):
        arrived(rx.at[a, 0], f_rs.at[a, n])

    @pl.when(core == 1)
    def _():
        pl.semaphore_wait(barrier, 8)
        tell(met)

    @pl.when(core == 0)
    def _():
        pl.semaphore_wait(met, 1)

    def own_slot(a, carry):
        @pl.when(sends_near(a))
        def _():
            own_after(a).start()

        own_over(a).start()
        return carry

    lax.fori_loop(0, SLOTS, own_slot, 0)

    def near_slot(a, carry):
        @pl.when(has_near(a))
        def _():
            came(a, 1)

            @pl.when(sends_near(a))
            def _():
                near_after(a).start()

            near_over(a).start()

        return carry

    lax.fori_loop(0, SLOTS, near_slot, 0)

    def far_slot(a):
        @pl.when((a < SLOTS) & has_far(a))
        def _():
            came(a, 3)
            far_over(a).start()

    far_slot(0)

    key_at = lax.broadcasted_iota(jnp.int32, (NKEY, HD), 0)
    lane8 = lax.broadcasted_iota(jnp.int32, (8, HD), 1)
    row_in = lane8 % GRP

    def dq_dst(a, j):
        return dq_ref.at[a, 0, :, pl.ds(pl.multiple_of(j * QW, QW), QW)]

    def send_dq(a, xs):
        for nc in range(2):
            j = 2 * xs + nc

            @pl.when(j == me)
            def _(j=j):
                pltpu.make_async_copy(dqs.at[a, j], dq_dst(a, me), dq_rs.at[0]).start()

            @pl.when(j != me)
            def _(j=j):
                remote(dqs.at[a, j], dq_dst(a, me), dq_ss.at[0], dq_rs.at[0], dev(j, y, c)).start()

    def held_dq():
        def each(n, carry):
            send_dq(n // NX, (x + 2 * (n % 2) + (n % NX) // 2) % NX)
            return carry

        lax.fori_loop(0, HOLD * NX, each, 0)

    def await_chunk(a, i):
        xs = (x + 2 * (i % 2) + i // 2) % NX
        for nc in range(2):
            for n, to in enumerate((qr, gr)):
                arrived(to.at[a, 2 * xs + nc], q_rs.at[n, a, 2 * xs + nc])
        return xs

    def chunk(a, xs, qc, gc, kc, vc, bias):
        off = 2 * xs + y
        for h in range(HPG):
            at = pl.ds(h * HD, HD)
            qc[pl.ds(h * GRP, GRP), :] = qr[a, pl.ds(2 * xs, 2), :, at].reshape(GRP, HD)
            gc[pl.ds(h * GRP, GRP), :] = gr[a, pl.ds(2 * xs, 2), :, at].reshape(GRP, HD)
        for t in range(17):
            at = off + t
            kc[pl.ds(t * GRP, GRP), :] = kv[0, a, at // 8, (at % 8) // 2, at % 2]
            vc[pl.ds(t * GRP, GRP), :] = kv[1, a, at // 8, (at % 8) // 2, at % 2]
        first = (a * NCTX + c) * 256 + off * GRP
        line = jnp.broadcast_to(start[pl.ds((a * NCTX + c) * 2 + off // 4, 1), :], (8, HD))
        line = pltpu.roll(line, (HD - GRP * (off % 4)) % HD, 1)
        line = jnp.where(lane8 < GRP, line, 0)
        line = line + pltpu.roll(line, GRP, 1)
        line = line + pltpu.roll(line, 2 * GRP, 1)
        low = jnp.maximum(line - (first - 512), row_in + 1)[:1]
        high = (row_in + 512)[:1]
        bias[...] = jnp.where((key_at >= low) & (key_at <= high), 0.0, -1e30)
        nt = (((1,), (1,)), ((), ()))
        scores = lax.dot_general(kc[...], qc[...], nt, preferred_element_type=jnp.float32)
        dweights = lax.dot_general(vc[...], gc[...], nt, preferred_element_type=jnp.float32)
        both = jnp.concatenate([bias[...]] * (STACK // HD), axis=1)
        scaled = scores * (FACTOR * LOG2E) + both
        top = jnp.max(scaled, axis=0, keepdims=True)
        exponent = jnp.exp2(scaled - top)
        total = jnp.sum(exponent, axis=0, keepdims=True)
        cross = jnp.sum(exponent * dweights, axis=0, keepdims=True)
        inverse = 1.0 / total
        weights = exponent * inverse
        dscores = (weights * (dweights - cross * inverse)).astype(jnp.bfloat16)
        weights = weights.astype(jnp.bfloat16)
        nn = (((1,), (0,)), ((), ()))
        dv = lax.dot_general(weights, gc[...], nn, preferred_element_type=jnp.float32)
        dk = lax.dot_general(dscores, qc[...], nn, preferred_element_type=jnp.float32)
        tn = (((0,), (0,)), ((), ()))
        dq = lax.dot_general(dscores, kc[...], tn, preferred_element_type=jnp.float32)
        acc[0, pl.ds(off, 17)] += dk.reshape(17, GRP, HD)
        acc[1, pl.ds(off, 17)] += dv.reshape(17, GRP, HD)
        dq = (dq * FACTOR).astype(jnp.bfloat16)
        for h in range(HPG):
            dqs[a, pl.ds(2 * xs, 2), :, pl.ds(h * HD, HD)] = dq[h * GRP : (h + 1) * GRP].reshape(2, ROWS, HD)

    def pair(a, i):
        both = [await_chunk(a, 2 * i), await_chunk(a, 2 * i + 1)]
        pl.when((a == HOLD) & (i == 0))(held_dq)
        for n, xs in enumerate(both):
            chunk(a, xs, *[ref.at[n] for ref in (qc, gc, kc, vc, bias)])
        for xs in both:
            pl.when(a >= HOLD)(functools.partial(send_dq, a, xs))

    def swap_copy(a, piece):
        return remote(dks.at[a, piece], rx.at[a, piece], dk_ss.at[a, piece], dk_rs.at[a, piece], over)

    def swap(a):
        for piece in range(3):
            for n, scale in enumerate((FACTOR, 1.0)):
                for xx in range(NX):
                    at = piece * 8 + 2 * xx
                    dko[a, piece, n, xx] = acc[n, at + halves[piece]] * scale
                    dks[a, piece, n, xx] = (acc[n, at + 1 - halves[piece]] * scale).astype(jnp.bfloat16)
            swap_copy(a, piece).start()

    def owner_copy(a, piece):
        hops = 2 - piece
        at = (a + SLOTS - 1 + (c + NCTX - hops) // NCTX) % SLOTS
        to = dev(me, halves[piece], hop(-hops))
        return remote(dsum.at[a, piece], own.at[at, piece], dk_ss.at[a, 3 + piece], dk_rs.at[at, 3 + piece], to)

    def pass_back(a):
        for piece in range(2):
            arrived(rx.at[a, piece], dk_rs.at[a, piece])
            dsum[a, piece] = (dko[a, piece] + rx[a, piece].astype(jnp.float32)).astype(jnp.bfloat16)
            owner_copy(a, piece).start()

    def slot(a, carry):
        far_slot(a + 1)
        came(a, 0)

        @pl.when(has_near(a))
        def _():
            came(a, 2)

        @pl.when(has_far(a))
        def _():
            came(a, 4)

        acc[...] = jnp.zeros_like(acc)

        def one(i, carry):
            pair(a, i)

            @pl.when((i == 0) & (a > 0))
            def _():
                pass_back(a - 1)

            return carry

        lax.fori_loop(0, NX // 2, one, 0)
        swap(a)
        return carry

    lax.fori_loop(0, SLOTS, slot, 0)

    for n, to in enumerate((qr, gr)):
        arrived(to.at[:, pl.ds(0, NJ - 1)], q_ss.at[n])
        arrived(kc.at[0, pl.ds(0, (NJ - 1) * SLOTS * ROWS)], a_ss.at[n])

    def sent_keys(a, carry):
        def sent(n):
            arrived(rx.at[a, 0], f_ss.at[a, n])

        sent(0)
        for n, when in ((1, sends_near(a)), (2, has_near(a)), (3, has_near(a) & sends_near(a)), (4, has_far(a))):
            pl.when(when)(functools.partial(sent, n))
        return carry

    lax.fori_loop(0, SLOTS, sent_keys, 0)

    def reduce(a, _):
        for n in (2, 3, 4):
            arrived(rx.at[a, 0], dk_rs.at[a, n])
        total = dko[a, 2] + rx[a, 2].astype(jnp.float32)
        for n in range(2):
            total = total + own[a, n].astype(jnp.float32)
        home[:, a] = total.astype(jnp.bfloat16)
        return _

    def home_src(n, j, at):
        return home.at[n, at, j // 2, pl.ds(pl.multiple_of((j % 2) * ROWS, ROWS), ROWS)]

    def home_dst(n, j, at):
        return (dk_ref, dv_ref)[n].at[at, 0, :, pl.ds(pl.multiple_of(j * HD, HD), HD)]

    def go_home(part):
        lax.fori_loop(2 * part, 2 * part + 2, reduce, 0)
        at = pl.ds(2 * part, 2)
        for p in PEERS:
            j = peer(*p)
            for n in range(2):
                remote(home_src(n, j, at), home_dst(n, me, at), h_ss.at[n], h_rs.at[n], dev(j, y, c)).start()
        for n in range(2):
            pltpu.make_async_copy(home_src(n, me, at), home_dst(n, me, at), h_rs.at[n]).start()

    go_home(0)
    pass_back(SLOTS - 1)
    go_home(1)

    def sent_grads(a, carry):
        for n in range(5):
            arrived(rx.at[a, 0], dk_ss.at[a, n])
        return carry

    lax.fori_loop(0, SLOTS, sent_grads, 0)
    arrived(dqs.at[:, pl.ds(0, NJ - 1)], dq_ss.at[0])
    arrived(dq_ref, dq_rs.at[0])
    for n, ref in enumerate((dk_ref, dv_ref)):
        arrived(kc.at[0, pl.ds(0, (NJ - 1) * SLOTS * ROWS)], h_ss.at[n])
        arrived(ref, h_rs.at[n])


def handed_on(dq, dk, dv, dq_out, dk_out, dv_out, dq_mid, dk_mid, dv_mid, sem):
    parts = [(dq, dq_mid, dq_out, a) for a in range(SLOTS)]
    parts += [(dk, dk_mid, dk_out, pl.ds(0, SLOTS)), (dv, dv_mid, dv_out, pl.ds(0, SLOTS))]
    ins = [pltpu.make_async_copy(r.at[at], m.at[at], sem.at[0, n]) for n, (r, m, _, at) in enumerate(parts)]
    outs = [pltpu.make_async_copy(m.at[at], o.at[at], sem.at[1, n]) for n, (_, m, o, at) in enumerate(parts)]
    for copy in ins:
        copy.start()
    for one, two in zip(ins, outs):
        one.wait()
        two.start()
    for copy in outs:
        copy.wait()


def body(queries, key_vectors, value_vectors, grad_output, doc_ids):
    bf, f32, dma = jnp.bfloat16, jnp.float32, pltpu.SemaphoreType.DMA
    hbm = pl.BlockSpec(memory_space=pltpu.HBM)
    vmem = pltpu.VMEM
    like = jax.ShapeDtypeStruct
    results = pl.pallas_call(
        kernel,
        out_shape=(
            like(queries.shape, bf),
            like(key_vectors.shape, bf),
            like(value_vectors.shape, bf),
        ),
        in_specs=[hbm] * 4 + [pl.BlockSpec(memory_space=vmem)],
        out_specs=(hbm,) * 3,
        scratch_shapes=[
            vmem((SLOTS, NJ, ROWS, QW), bf),
            vmem((SLOTS, NJ, ROWS, QW), bf),
            vmem((SLOTS, NJ, ROWS, QW), bf),
            vmem((2, SLOTS, 3, NX, 2, GRP, HD), bf),
            vmem((2, STACK, HD), bf),
            vmem((2, STACK, HD), bf),
            vmem((2, NKEY, HD), bf),
            vmem((2, NKEY, HD), bf),
            vmem((2, NKEY, HD), f32),
            vmem((HD, HD), jnp.int32),
            vmem((2, 24, GRP, HD), f32),
            vmem((SLOTS, 3, 2, NX, GRP, HD), bf),
            vmem((SLOTS, 3, 2, NX, GRP, HD), f32),
            vmem((SLOTS, 3, 2, NX, GRP, HD), bf),
            vmem((SLOTS, 2, 2, NX, GRP, HD), bf),
            vmem((SLOTS, 2, 2, NX, GRP, HD), bf),
            vmem((2, SLOTS, NX, GRP, HD), bf),
            dma((2,)),
            dma((2, SLOTS, NJ)),
            dma((2,)),
            dma((2,)),
            dma((SLOTS, 5)),
            dma((SLOTS, 5)),
            dma((1,)),
            dma((1,)),
            dma((SLOTS, 5)),
            dma((SLOTS, 5)),
            dma((2,)),
            dma((2,)),
            pltpu.SemaphoreType.REGULAR,
        ],
        compiler_params=pltpu.CompilerParams(
            collective_id=0, has_side_effects=True, vmem_limit_bytes=62 << 20
        ),
    )(queries, key_vectors, value_vectors, grad_output, doc_ids.reshape(HD, HD))
    return pl.pallas_call(
        handed_on,
        out_shape=tuple(like(r.shape, bf) for r in results),
        in_specs=[hbm] * 3,
        out_specs=(hbm,) * 3,
        scratch_shapes=[vmem(r.shape, bf) for r in results] + [dma((2, 6))],
    )(*results)


def solution(mesh):
    placed = P(None, "ctx", "head", None)
    return jax.shard_map(
        body,
        mesh=mesh,
        in_specs=(placed,) * 4 + (P(),),
        out_specs=(placed,) * 3,
        check_vma=False,
    )
```

```python
import functools
import math

import jax
import jax.numpy as jnp
from jax import lax
from jax.experimental import pallas as pl
from jax.experimental.pallas import tpu as pltpu
from jax.sharding import PartitionSpec as P

MESH = pl.DeviceIdType.MESH
HD = 128
NX = 4
NJ = 8
NCTX = 16
NZ = 8
SLOTS = 4
ROWS = 16
GRP = 32
HPG = 12
QW = HPG * HD
NKEY = 17 * GRP
STACK = HPG * GRP
HOLD = 2
LOG2E = 1.4426950408889634
FACTOR = 1.0 / math.sqrt(HD)
PEERS = tuple((dx, dc) for dx in (2, 1, 3, 0) for dc in (0, 1) if (dx, dc) != (0, 0))


def kernel(
    q_ref, k_ref, v_ref, g_ref, doc_ref, dq_ref, dk_ref, dv_ref,
    qr, gr, dqs, kv, qc, gc, kc, vc, bias, band, start, acc, dks, dko, rx, dsum, own, home,
    q_ss, q_rs, a_ss, a_rs, f_ss, f_rs, dq_ss, dq_rs, dk_ss, dk_rs, h_ss, h_rs, met,
):
    head = lax.axis_index("head")
    c = lax.axis_index("ctx")
    x, y, core = head // 4, (head // 2) % 2, head % 2
    me = x * 2 + core
    other = 1 - y

    def dev(nj, ny, nc):
        return dict(head=(nj // 2) * 4 + ny * 2 + nj % 2, ctx=nc)

    def hop(by):
        return (c + by + NCTX) % NCTX

    def peer(dx, dc):
        return ((x + dx) % NX) * 2 + (core + dc) % 2

    def remote(src, dst, ss, rs, to):
        return pltpu.make_async_remote_copy(
            src_ref=src, dst_ref=dst, send_sem=ss, recv_sem=rs, device_id=to, device_id_type=MESH
        )

    def arrived(ref, sem):
        pltpu.make_async_copy(ref, ref, sem).wait()

    z = c % NZ
    barrier = pltpu.get_barrier_semaphore()
    over = dev(me, other, c)
    after = dev(me, (y + (z + 1) // NZ) % 2, hop(1))

    def announce(to):
        pl.semaphore_signal(barrier, inc=1, device_id=to, device_id_type=MESH)

    for dx in range(1, NX):
        announce(dev(((x + dx) % NX) * 2, y, c))

    @pl.when(core == 1)
    def _():
        announce(dev(2 * x, y, c))

    y_before, y_two = (y + 1 - (z + NZ - 1) // NZ) % 2, (y + (z + 2) // NZ) % 2
    for ny, by in ((other, 0), ((y + (z + 1) // NZ) % 2, 1), (y_before, -1), (y_two, 2)):
        announce(dev(2 * x + 1, ny, hop(by)))

    def tell(sem):
        pl.semaphore_signal(sem, inc=1, device_id=dev(2 * x + 1 - core, y, c), device_id_type=MESH)

    @pl.when(core == 0)
    def _():
        pl.semaphore_wait(barrier, NJ - 1)
        tell(met)

    @pl.when(core == 1)
    def _():
        pl.semaphore_wait(met, 1)

    def kv_src(ref, j):
        return ref.at[:, 0, :, pl.ds(pl.multiple_of(j * HD, HD), HD)]

    def kv_dst(n, j):
        return kv.at[n, :, 2, j // 2, y, pl.ds(pl.multiple_of((j % 2) * ROWS, ROWS), ROWS)]

    for p in PEERS:
        j = peer(*p)
        for n, ref in enumerate((k_ref, v_ref)):
            remote(kv_src(ref, j), kv_dst(n, me), a_ss.at[n], a_rs.at[n], dev(j, y, c)).start()
    for n, ref in enumerate((k_ref, v_ref)):
        pltpu.make_async_copy(kv_src(ref, me), kv_dst(n, me), a_rs.at[n]).start()

    def q_src(ref, a, j):
        return ref.at[a, 0, :, pl.ds(pl.multiple_of(j * QW, QW), QW)]

    def send_q(a):
        for p in PEERS:
            j = peer(*p)
            for n, (ref, to) in enumerate(((q_ref, qr), (g_ref, gr))):
                remote(q_src(ref, a, j), to.at[a, me], q_ss.at[n], q_rs.at[n, a, me], dev(j, y, c)).start()
        for n, (ref, to) in enumerate(((q_ref, qr), (g_ref, gr))):
            pltpu.make_async_copy(q_src(ref, a, me), to.at[a, me], q_rs.at[n, a, me]).start()

    send_q(0)

    send_q(1)

    for n in range(2):
        arrived(kv.at[n, :, 2, :, y], a_rs.at[n])
    step = (c + 1) // NCTX
    halves = ((y + 1 - (z + NZ - 2) // NZ) % 2, (y + 1 - (z + NZ - 1) // NZ) % 2, y)

    def half(a, piece, of):
        return kv.at[:, a, piece, :, halves[of]]

    for first, piece in ((0, 0), (0, 1), (1, 0)):

        @pl.when(c == first)
        def _(piece=piece):
            kv[:, 0, piece] = jnp.zeros((2, NX, 2, GRP, HD), jnp.bfloat16)

    def sends_near(a):
        return (c < NCTX - 1) | (a < SLOTS - 1)

    def has_near(a):
        return (c > 0) | (a > 0)

    def has_far(a):
        return (c > 1) | (a > 0)

    def own_over(a):
        return remote(half(a, 2, 2), half(a, 2, 2), f_ss.at[a, 0], f_rs.at[a, 0], over)

    def own_after(a):
        at = (a + step) % SLOTS
        return remote(half(a, 2, 2), half(at, 1, 2), f_ss.at[a, 1], f_rs.at[at, 1], after)

    def near_after(a):
        at = (a + step) % SLOTS
        return remote(half(a, 1, 1), half(at, 0, 1), f_ss.at[a, 3], f_rs.at[at, 3], after)

    def near_over(a):
        return remote(half(a, 1, 1), half(a, 1, 1), f_ss.at[a, 2], f_rs.at[a, 2], over)

    def far_over(a):
        return remote(half(a, 0, 0), half(a, 0, 0), f_ss.at[a, 4], f_rs.at[a, 4], over)

    def came(a, n):
        arrived(rx.at[a, 0], f_rs.at[a, n])

    @pl.when(core == 1)
    def _():
        pl.semaphore_wait(barrier, 8)
        tell(met)

    @pl.when(core == 0)
    def _():
        pl.semaphore_wait(met, 1)

    def own_slot(a):
        @pl.when(sends_near(a))
        def _():
            own_after(a).start()

        own_over(a).start()

    def near_slot(a):
        @pl.when(has_near(a))
        def _():
            came(a, 1)

            @pl.when(sends_near(a))
            def _():
                near_after(a).start()

            near_over(a).start()

    def far_slot(a):
        @pl.when((a < SLOTS) & has_far(a))
        def _():
            came(a, 3)
            far_over(a).start()

    own_slot(0)
    own_slot(1)
    send_q(2)
    send_q(3)

    doc = doc_ref[...]
    row = lax.broadcasted_iota(jnp.int32, doc.shape, 0)
    lane = lax.broadcasted_iota(jnp.int32, doc.shape, 1)
    before = pltpu.roll(doc, 1, 1)
    before = jnp.where(lane == 0, pltpu.roll(before, 1, 0), before)
    run = jnp.where(doc != before, row * HD + lane, 0)
    for s in (1, 2, 4, 8, 16, 32, 64):
        run = jnp.maximum(run, jnp.where(lane >= s, pltpu.roll(run, s, 1), 0))
    last = jnp.broadcast_to(jnp.max(run, axis=1, keepdims=True), doc.shape)
    carry = jnp.where(row >= 1, pltpu.roll(last, 1, 0), 0)
    for s in (1, 2, 4, 8, 16, 32, 64):
        carry = jnp.maximum(carry, jnp.where(row >= s, pltpu.roll(carry, s, 0), 0))
    start[...] = jnp.maximum(run, carry)

    near_slot(0)
    own_slot(2)
    near_slot(1)
    far_slot(0)
    own_slot(3)

    key_at = lax.broadcasted_iota(jnp.int32, (NKEY, HD), 0)
    lane8 = lax.broadcasted_iota(jnp.int32, (8, HD), 1)
    ahead = key_at - lax.broadcasted_iota(jnp.int32, (NKEY, HD), 1) % GRP
    band[...] = jnp.where((ahead > 0) & (ahead <= 512), 0.0, -1e30)

    def dq_dst(a, j):
        return dq_ref.at[a, 0, :, pl.ds(pl.multiple_of(j * QW, QW), QW)]

    def send_dq(a, xs):
        for nc in range(2):
            j = 2 * xs + nc

            @pl.when(j == me)
            def _(j=j):
                pltpu.make_async_copy(dqs.at[a, j], dq_dst(a, me), dq_rs.at[0]).start()

            @pl.when(j != me)
            def _(j=j):
                remote(dqs.at[a, j], dq_dst(a, me), dq_ss.at[0], dq_rs.at[0], dev(j, y, c)).start()

    def held_dq():
        def each(n, carry):
            send_dq(n // NX, (x + 2 * (n % 2) + (n % NX) // 2) % NX)
            return carry

        lax.fori_loop(0, HOLD * NX, each, 0)

    def await_chunk(a, i):
        xs = (x + 2 * (i % 2) + i // 2) % NX
        for nc in range(2):
            for n, to in enumerate((qr, gr)):
                arrived(to.at[a, 2 * xs + nc], q_rs.at[n, a, 2 * xs + nc])
        return xs

    def chunk(a, xs, qc, gc, kc, vc, bias):
        off = 2 * xs + y
        for h in range(HPG):
            at = pl.ds(h * HD, HD)
            qc[pl.ds(h * GRP, GRP), :] = qr[a, pl.ds(2 * xs, 2), :, at].reshape(GRP, HD)
            gc[pl.ds(h * GRP, GRP), :] = gr[a, pl.ds(2 * xs, 2), :, at].reshape(GRP, HD)
        for t in range(17):
            at = off + t
            kc[pl.ds(t * GRP, GRP), :] = kv[0, a, at // 8, (at % 8) // 2, at % 2]
            vc[pl.ds(t * GRP, GRP), :] = kv[1, a, at // 8, (at % 8) // 2, at % 2]
        first = (a * NCTX + c) * 256 + off * GRP
        line = jnp.broadcast_to(start[pl.ds((a * NCTX + c) * 2 + off // 4, 1), :], (8, HD))
        line = pltpu.roll(line, (HD - GRP * (off % 4)) % HD, 1)
        line = jnp.where(lane8 < GRP, line, 0)
        line = line + pltpu.roll(line, GRP, 1)
        line = line + pltpu.roll(line, 2 * GRP, 1)
        bias[...] = jnp.where(key_at >= (line - (first - 512))[:1], band[...], -1e30)
        nt = (((1,), (1,)), ((), ()))
        scores = lax.dot_general(kc[...], qc[...], nt, preferred_element_type=jnp.float32)
        dweights = lax.dot_general(vc[...], gc[...], nt, preferred_element_type=jnp.float32)
        both = jnp.concatenate([bias[...]] * (STACK // HD), axis=1)
        scaled = scores * (FACTOR * LOG2E) + both
        top = jnp.max(scaled, axis=0, keepdims=True)
        exponent = jnp.exp2(scaled - top)
        total = jnp.sum(exponent, axis=0, keepdims=True)
        cross = jnp.sum(exponent * dweights, axis=0, keepdims=True)
        inverse = 1.0 / total
        weights = exponent * inverse
        dscores = (weights * (dweights - cross * inverse)).astype(jnp.bfloat16)
        weights = weights.astype(jnp.bfloat16)
        nn = (((1,), (0,)), ((), ()))
        dv = lax.dot_general(weights, gc[...], nn, preferred_element_type=jnp.float32)
        dk = lax.dot_general(dscores, qc[...], nn, preferred_element_type=jnp.float32)
        tn = (((0,), (0,)), ((), ()))
        dq = lax.dot_general(dscores, kc[...], tn, preferred_element_type=jnp.float32)
        acc[0, pl.ds(off, 17)] += dk.reshape(17, GRP, HD)
        acc[1, pl.ds(off, 17)] += dv.reshape(17, GRP, HD)
        dq = (dq * FACTOR).astype(jnp.bfloat16)
        for h in range(HPG):
            dqs[a, pl.ds(2 * xs, 2), :, pl.ds(h * HD, HD)] = dq[h * GRP : (h + 1) * GRP].reshape(2, ROWS, HD)

    def pair(a, i):
        both = [await_chunk(a, 2 * i), await_chunk(a, 2 * i + 1)]
        pl.when((a == HOLD) & (i == 0))(held_dq)
        for n, xs in enumerate(both):
            chunk(a, xs, *[ref.at[n] for ref in (qc, gc, kc, vc, bias)])
        for xs in both:
            pl.when(a >= HOLD)(functools.partial(send_dq, a, xs))

    def swap_copy(a, piece):
        return remote(dks.at[a, piece], rx.at[a, piece], dk_ss.at[a, piece], dk_rs.at[a, piece], over)

    def swap(a):
        for piece in range(3):
            for n, scale in enumerate((FACTOR, 1.0)):
                for xx in range(NX):
                    at = piece * 8 + 2 * xx
                    dko[a, piece, n, xx] = acc[n, at + halves[piece]] * scale
                    dks[a, piece, n, xx] = (acc[n, at + 1 - halves[piece]] * scale).astype(jnp.bfloat16)
            swap_copy(a, piece).start()

    def owner_copy(a, piece):
        hops = 2 - piece
        at = (a + SLOTS - 1 + (c + NCTX - hops) // NCTX) % SLOTS
        to = dev(me, halves[piece], hop(-hops))
        return remote(dsum.at[a, piece], own.at[at, piece], dk_ss.at[a, 3 + piece], dk_rs.at[at, 3 + piece], to)

    def pass_back(a):
        for piece in range(2):
            arrived(rx.at[a, piece], dk_rs.at[a, piece])
            dsum[a, piece] = (dko[a, piece] + rx[a, piece].astype(jnp.float32)).astype(jnp.bfloat16)
            owner_copy(a, piece).start()

    def slot(a, carry):
        came(a, 0)

        @pl.when(has_near(a))
        def _():
            came(a, 2)

        @pl.when(has_far(a))
        def _():
            came(a, 4)

        acc[...] = jnp.zeros_like(acc)

        def one(i, carry):
            pair(a, i)

            @pl.when(i == 0)
            def _():
                far_slot(a + 1)

            @pl.when(a == 0)
            def _():
                near_slot(2 + i)

            @pl.when((i == 0) & (a > 0))
            def _():
                pass_back(a - 1)

            return carry

        lax.fori_loop(0, NX // 2, one, 0)
        swap(a)
        return carry

    lax.fori_loop(0, SLOTS, slot, 0)

    for n, to in enumerate((qr, gr)):
        arrived(to.at[:, pl.ds(0, NJ - 1)], q_ss.at[n])
        arrived(kc.at[0, pl.ds(0, (NJ - 1) * SLOTS * ROWS)], a_ss.at[n])

    def sent_keys(a, carry):
        def sent(n):
            arrived(rx.at[a, 0], f_ss.at[a, n])

        sent(0)
        for n, when in ((1, sends_near(a)), (2, has_near(a)), (3, has_near(a) & sends_near(a)), (4, has_far(a))):
            pl.when(when)(functools.partial(sent, n))
        return carry

    lax.fori_loop(0, SLOTS, sent_keys, 0)

    def reduce(a, _):
        for n in (2, 3, 4):
            arrived(rx.at[a, 0], dk_rs.at[a, n])
        total = dko[a, 2] + rx[a, 2].astype(jnp.float32)
        for n in range(2):
            total = total + own[a, n].astype(jnp.float32)
        home[:, a] = total.astype(jnp.bfloat16)
        return _

    def home_src(n, j, at):
        return home.at[n, at, j // 2, pl.ds(pl.multiple_of((j % 2) * ROWS, ROWS), ROWS)]

    def home_dst(n, j, at):
        return (dk_ref, dv_ref)[n].at[at, 0, :, pl.ds(pl.multiple_of(j * HD, HD), HD)]

    def go_home(part):
        lax.fori_loop(2 * part, 2 * part + 2, reduce, 0)
        at = pl.ds(2 * part, 2)
        for p in PEERS:
            j = peer(*p)
            for n in range(2):
                remote(home_src(n, j, at), home_dst(n, me, at), h_ss.at[n], h_rs.at[n], dev(j, y, c)).start()
        for n in range(2):
            pltpu.make_async_copy(home_src(n, me, at), home_dst(n, me, at), h_rs.at[n]).start()

    go_home(0)
    pass_back(SLOTS - 1)
    go_home(1)

    def sent_grads(a, carry):
        for n in range(5):
            arrived(rx.at[a, 0], dk_ss.at[a, n])
        return carry

    lax.fori_loop(0, SLOTS, sent_grads, 0)
    arrived(dqs.at[:, pl.ds(0, NJ - 1)], dq_ss.at[0])
    arrived(dq_ref, dq_rs.at[0])
    for n, ref in enumerate((dk_ref, dv_ref)):
        arrived(kc.at[0, pl.ds(0, (NJ - 1) * SLOTS * ROWS)], h_ss.at[n])
        arrived(ref, h_rs.at[n])


def handed_on(dq, dk, dv, dq_out, dk_out, dv_out, dq_mid, dk_mid, dv_mid, sem):
    parts = [(dq, dq_mid, dq_out, a) for a in range(SLOTS)]
    parts += [(dk, dk_mid, dk_out, pl.ds(0, SLOTS)), (dv, dv_mid, dv_out, pl.ds(0, SLOTS))]
    ins = [pltpu.make_async_copy(r.at[at], m.at[at], sem.at[0, n]) for n, (r, m, _, at) in enumerate(parts)]
    outs = [pltpu.make_async_copy(m.at[at], o.at[at], sem.at[1, n]) for n, (_, m, o, at) in enumerate(parts)]
    for copy in ins:
        copy.start()
    for one, two in zip(ins, outs):
        one.wait()
        two.start()
    for copy in outs:
        copy.wait()


def body(queries, key_vectors, value_vectors, grad_output, doc_ids):
    bf, f32, dma = jnp.bfloat16, jnp.float32, pltpu.SemaphoreType.DMA
    hbm = pl.BlockSpec(memory_space=pltpu.HBM)
    vmem = pltpu.VMEM
    like = jax.ShapeDtypeStruct
    results = pl.pallas_call(
        kernel,
        out_shape=(
            like(queries.shape, bf),
            like(key_vectors.shape, bf),
            like(value_vectors.shape, bf),
        ),
        in_specs=[hbm] * 4 + [pl.BlockSpec(memory_space=vmem)],
        out_specs=(hbm,) * 3,
        scratch_shapes=[
            vmem((SLOTS, NJ, ROWS, QW), bf),
            vmem((SLOTS, NJ, ROWS, QW), bf),
            vmem((SLOTS, NJ, ROWS, QW), bf),
            vmem((2, SLOTS, 3, NX, 2, GRP, HD), bf),
            vmem((2, STACK, HD), bf),
            vmem((2, STACK, HD), bf),
            vmem((2, NKEY, HD), bf),
            vmem((2, NKEY, HD), bf),
            vmem((2, NKEY, HD), f32),
            vmem((NKEY, HD), f32),
            vmem((HD, HD), jnp.int32),
            vmem((2, 24, GRP, HD), f32),
            vmem((SLOTS, 3, 2, NX, GRP, HD), bf),
            vmem((SLOTS, 3, 2, NX, GRP, HD), f32),
            vmem((SLOTS, 3, 2, NX, GRP, HD), bf),
            vmem((SLOTS, 2, 2, NX, GRP, HD), bf),
            vmem((SLOTS, 2, 2, NX, GRP, HD), bf),
            vmem((2, SLOTS, NX, GRP, HD), bf),
            dma((2,)),
            dma((2, SLOTS, NJ)),
            dma((2,)),
            dma((2,)),
            dma((SLOTS, 5)),
            dma((SLOTS, 5)),
            dma((1,)),
            dma((1,)),
            dma((SLOTS, 5)),
            dma((SLOTS, 5)),
            dma((2,)),
            dma((2,)),
            pltpu.SemaphoreType.REGULAR,
        ],
        compiler_params=pltpu.CompilerParams(
            collective_id=0, has_side_effects=True, vmem_limit_bytes=62 << 20
        ),
    )(queries, key_vectors, value_vectors, grad_output, doc_ids.reshape(HD, HD))
    return pl.pallas_call(
        handed_on,
        out_shape=tuple(like(r.shape, bf) for r in results),
        in_specs=[hbm] * 3,
        out_specs=(hbm,) * 3,
        scratch_shapes=[vmem(r.shape, bf) for r in results] + [dma((2, 6))],
    )(*results)


def solution(mesh):
    placed = P(None, "ctx", "head", None)
    return jax.shard_map(
        body,
        mesh=mesh,
        in_specs=(placed,) * 4 + (P(),),
        out_specs=(placed,) * 3,
        check_vma=False,
    )
```

```python
import functools
import math

import jax
import jax.numpy as jnp
from jax import lax
from jax.experimental import pallas as pl
from jax.experimental.pallas import tpu as pltpu
from jax.sharding import PartitionSpec as P

MESH = pl.DeviceIdType.MESH
HD = 128
NX = 4
NJ = 8
NCTX = 16
NZ = 8
SLOTS = 4
ROWS = 16
GRP = 32
HPG = 12
QW = HPG * HD
NKEY = 17 * GRP
STACK = HPG * GRP
HOLD = 2
LOG2E = 1.4426950408889634
FACTOR = 1.0 / math.sqrt(HD)
PEERS = tuple((dx, dc) for dx in (2, 1, 3, 0) for dc in (0, 1) if (dx, dc) != (0, 0))


def kernel(
    q_ref, k_ref, v_ref, g_ref, doc_ref, dq_ref, dk_ref, dv_ref,
    qr, gr, dqs, kv, qc, gc, kc, vc, bias, band, start, acc, dks, dko, rx, dsum, own, home,
    q_ss, q_rs, a_ss, a_rs, f_ss, f_rs, dq_ss, dq_rs, dk_ss, dk_rs, h_ss, h_rs, met,
):
    head = lax.axis_index("head")
    c = lax.axis_index("ctx")
    x, y, core = head // 4, (head // 2) % 2, head % 2
    me = x * 2 + core
    other = 1 - y

    def dev(nj, ny, nc):
        return dict(head=(nj // 2) * 4 + ny * 2 + nj % 2, ctx=nc)

    def hop(by):
        return (c + by + NCTX) % NCTX

    def peer(dx, dc):
        return ((x + dx) % NX) * 2 + (core + dc) % 2

    def remote(src, dst, ss, rs, to):
        return pltpu.make_async_remote_copy(
            src_ref=src, dst_ref=dst, send_sem=ss, recv_sem=rs, device_id=to, device_id_type=MESH
        )

    def arrived(ref, sem):
        pltpu.make_async_copy(ref, ref, sem).wait()

    z = c % NZ
    barrier = pltpu.get_barrier_semaphore()
    over = dev(me, other, c)
    after = dev(me, (y + (z + 1) // NZ) % 2, hop(1))

    def announce(to):
        pl.semaphore_signal(barrier, inc=1, device_id=to, device_id_type=MESH)

    for dx in range(1, NX):
        announce(dev(((x + dx) % NX) * 2, y, c))

    @pl.when(core == 1)
    def _():
        announce(dev(2 * x, y, c))

    y_before, y_two = (y + 1 - (z + NZ - 1) // NZ) % 2, (y + (z + 2) // NZ) % 2
    for ny, by in ((other, 0), ((y + (z + 1) // NZ) % 2, 1), (y_before, -1), (y_two, 2)):
        announce(dev(2 * x + 1, ny, hop(by)))

    def kv_src(ref, j):
        return ref.at[:, 0, :, pl.ds(pl.multiple_of(j * HD, HD), HD)]

    def kv_dst(n, j):
        return kv.at[n, :, 2, j // 2, y, pl.ds(pl.multiple_of((j % 2) * ROWS, ROWS), ROWS)]

    def q_src(ref, a, j):
        return ref.at[a, 0, :, pl.ds(pl.multiple_of(j * QW, QW), QW)]

    for n, ref in enumerate((k_ref, v_ref)):
        pltpu.make_async_copy(kv_src(ref, me), kv_dst(n, me), a_rs.at[n]).start()
    for a in range(SLOTS):
        for n, (ref, to) in enumerate(((q_ref, qr), (g_ref, gr))):
            pltpu.make_async_copy(q_src(ref, a, me), to.at[a, me], q_rs.at[n, a, me]).start()

    doc = doc_ref[...]
    row = lax.broadcasted_iota(jnp.int32, doc.shape, 0)
    lane = lax.broadcasted_iota(jnp.int32, doc.shape, 1)
    before = pltpu.roll(doc, 1, 1)
    before = jnp.where(lane == 0, pltpu.roll(before, 1, 0), before)
    run = jnp.where(doc != before, row * HD + lane, 0)
    for s in (1, 2, 4, 8, 16, 32, 64):
        run = jnp.maximum(run, jnp.where(lane >= s, pltpu.roll(run, s, 1), 0))
    last = jnp.broadcast_to(jnp.max(run, axis=1, keepdims=True), doc.shape)
    carry = jnp.where(row >= 1, pltpu.roll(last, 1, 0), 0)
    for s in (1, 2, 4, 8, 16, 32, 64):
        carry = jnp.maximum(carry, jnp.where(row >= s, pltpu.roll(carry, s, 0), 0))
    start[...] = jnp.maximum(run, carry)

    key_at = lax.broadcasted_iota(jnp.int32, (NKEY, HD), 0)
    ahead = key_at - lax.broadcasted_iota(jnp.int32, (NKEY, HD), 1) % GRP
    band[...] = jnp.where((ahead > 0) & (ahead <= 512), 0.0, -1e30)

    for first, piece in ((0, 0), (0, 1), (1, 0)):

        @pl.when(c == first)
        def _(piece=piece):
            kv[:, 0, piece] = jnp.zeros((2, NX, 2, GRP, HD), jnp.bfloat16)

    def tell(sem):
        pl.semaphore_signal(sem, inc=1, device_id=dev(2 * x + 1 - core, y, c), device_id_type=MESH)

    @pl.when(core == 0)
    def _():
        pl.semaphore_wait(barrier, NJ - 1)
        tell(met)

    @pl.when(core == 1)
    def _():
        pl.semaphore_wait(met, 1)

    for p in PEERS:
        j = peer(*p)
        for n, ref in enumerate((k_ref, v_ref)):
            remote(kv_src(ref, j), kv_dst(n, me), a_ss.at[n], a_rs.at[n], dev(j, y, c)).start()

    def send_q(a):
        for p in PEERS:
            j = peer(*p)
            for n, (ref, to) in enumerate(((q_ref, qr), (g_ref, gr))):
                remote(q_src(ref, a, j), to.at[a, me], q_ss.at[n], q_rs.at[n, a, me], dev(j, y, c)).start()

    send_q(0)

    send_q(1)

    for n in range(2):
        arrived(kv.at[n, :, 2, :, y], a_rs.at[n])
    step = (c + 1) // NCTX
    halves = ((y + 1 - (z + NZ - 2) // NZ) % 2, (y + 1 - (z + NZ - 1) // NZ) % 2, y)

    def half(a, piece, of):
        return kv.at[:, a, piece, :, halves[of]]

    def sends_near(a):
        return (c < NCTX - 1) | (a < SLOTS - 1)

    def has_near(a):
        return (c > 0) | (a > 0)

    def has_far(a):
        return (c > 1) | (a > 0)

    def own_over(a):
        return remote(half(a, 2, 2), half(a, 2, 2), f_ss.at[a, 0], f_rs.at[a, 0], over)

    def own_after(a):
        at = (a + step) % SLOTS
        return remote(half(a, 2, 2), half(at, 1, 2), f_ss.at[a, 1], f_rs.at[at, 1], after)

    def near_after(a):
        at = (a + step) % SLOTS
        return remote(half(a, 1, 1), half(at, 0, 1), f_ss.at[a, 3], f_rs.at[at, 3], after)

    def near_over(a):
        return remote(half(a, 1, 1), half(a, 1, 1), f_ss.at[a, 2], f_rs.at[a, 2], over)

    def far_over(a):
        return remote(half(a, 0, 0), half(a, 0, 0), f_ss.at[a, 4], f_rs.at[a, 4], over)

    def came(a, n):
        arrived(rx.at[a, 0], f_rs.at[a, n])

    @pl.when(core == 1)
    def _():
        pl.semaphore_wait(barrier, 8)
        tell(met)

    @pl.when(core == 0)
    def _():
        pl.semaphore_wait(met, 1)

    def own_slot(a):
        @pl.when(sends_near(a))
        def _():
            own_after(a).start()

        own_over(a).start()

    def near_slot(a):
        @pl.when(has_near(a))
        def _():
            came(a, 1)

            @pl.when(sends_near(a))
            def _():
                near_after(a).start()

            near_over(a).start()

    def far_slot(a):
        @pl.when((a < SLOTS) & has_far(a))
        def _():
            came(a, 3)
            far_over(a).start()

    own_slot(0)
    own_slot(1)
    send_q(2)
    send_q(3)

    near_slot(0)
    own_slot(2)
    near_slot(1)
    far_slot(0)
    own_slot(3)

    lane8 = lax.broadcasted_iota(jnp.int32, (8, HD), 1)

    def dq_dst(a, j):
        return dq_ref.at[a, 0, :, pl.ds(pl.multiple_of(j * QW, QW), QW)]

    def send_dq(a, xs):
        for nc in range(2):
            j = 2 * xs + nc

            @pl.when(j == me)
            def _(j=j):
                pltpu.make_async_copy(dqs.at[a, j], dq_dst(a, me), dq_rs.at[0]).start()

            @pl.when(j != me)
            def _(j=j):
                remote(dqs.at[a, j], dq_dst(a, me), dq_ss.at[0], dq_rs.at[0], dev(j, y, c)).start()

    def held_dq():
        def each(n, carry):
            send_dq(n // NX, (x + 2 * (n % 2) + (n % NX) // 2) % NX)
            return carry

        lax.fori_loop(0, HOLD * NX, each, 0)

    def await_chunk(a, i):
        xs = (x + 2 * (i % 2) + i // 2) % NX
        for nc in range(2):
            for n, to in enumerate((qr, gr)):
                arrived(to.at[a, 2 * xs + nc], q_rs.at[n, a, 2 * xs + nc])
        return xs

    def chunk(a, xs, qc, gc, kc, vc, bias):
        off = 2 * xs + y
        for h in range(HPG):
            at = pl.ds(h * HD, HD)
            qc[pl.ds(h * GRP, GRP), :] = qr[a, pl.ds(2 * xs, 2), :, at].reshape(GRP, HD)
            gc[pl.ds(h * GRP, GRP), :] = gr[a, pl.ds(2 * xs, 2), :, at].reshape(GRP, HD)
        for t in range(17):
            at = off + t
            kc[pl.ds(t * GRP, GRP), :] = kv[0, a, at // 8, (at % 8) // 2, at % 2]
            vc[pl.ds(t * GRP, GRP), :] = kv[1, a, at // 8, (at % 8) // 2, at % 2]
        first = (a * NCTX + c) * 256 + off * GRP
        line = jnp.broadcast_to(start[pl.ds((a * NCTX + c) * 2 + off // 4, 1), :], (8, HD))
        line = pltpu.roll(line, (HD - GRP * (off % 4)) % HD, 1)
        line = jnp.where(lane8 < GRP, line, 0)
        line = line + pltpu.roll(line, GRP, 1)
        line = line + pltpu.roll(line, 2 * GRP, 1)
        bias[...] = jnp.where(key_at >= (line - (first - 512))[:1], band[...], -1e30)
        nt = (((1,), (1,)), ((), ()))
        scores = lax.dot_general(kc[...], qc[...], nt, preferred_element_type=jnp.float32)
        dweights = lax.dot_general(vc[...], gc[...], nt, preferred_element_type=jnp.float32)
        both = jnp.concatenate([bias[...]] * (STACK // HD), axis=1)
        scaled = scores * (FACTOR * LOG2E) + both
        top = jnp.max(scaled, axis=0, keepdims=True)
        exponent = jnp.exp2(scaled - top)
        total = jnp.sum(exponent, axis=0, keepdims=True)
        cross = jnp.sum(exponent * dweights, axis=0, keepdims=True)
        inverse = 1.0 / total
        weights = exponent * inverse
        dscores = (weights * (dweights - cross * inverse)).astype(jnp.bfloat16)
        weights = weights.astype(jnp.bfloat16)
        nn = (((1,), (0,)), ((), ()))
        dv = lax.dot_general(weights, gc[...], nn, preferred_element_type=jnp.float32)
        dk = lax.dot_general(dscores, qc[...], nn, preferred_element_type=jnp.float32)
        tn = (((0,), (0,)), ((), ()))
        dq = lax.dot_general(dscores, kc[...], tn, preferred_element_type=jnp.float32)
        acc[0, pl.ds(off, 17)] += dk.reshape(17, GRP, HD)
        acc[1, pl.ds(off, 17)] += dv.reshape(17, GRP, HD)
        dq = (dq * FACTOR).astype(jnp.bfloat16)
        for h in range(HPG):
            dqs[a, pl.ds(2 * xs, 2), :, pl.ds(h * HD, HD)] = dq[h * GRP : (h + 1) * GRP].reshape(2, ROWS, HD)

    def pair(a, i):
        both = [await_chunk(a, 2 * i), await_chunk(a, 2 * i + 1)]
        pl.when((a == HOLD) & (i == 0))(held_dq)
        for n, xs in enumerate(both):
            chunk(a, xs, *[ref.at[n] for ref in (qc, gc, kc, vc, bias)])
        for xs in both:
            pl.when(a >= HOLD)(functools.partial(send_dq, a, xs))

    def swap_copy(a, piece):
        return remote(dks.at[a, piece], rx.at[a, piece], dk_ss.at[a, piece], dk_rs.at[a, piece], over)

    def swap(a):
        for piece in range(3):
            for n, scale in enumerate((FACTOR, 1.0)):
                for xx in range(NX):
                    at = piece * 8 + 2 * xx
                    dko[a, piece, n, xx] = acc[n, at + halves[piece]] * scale
                    dks[a, piece, n, xx] = (acc[n, at + 1 - halves[piece]] * scale).astype(jnp.bfloat16)
            swap_copy(a, piece).start()

    def owner_copy(a, piece):
        hops = 2 - piece
        at = (a + SLOTS - 1 + (c + NCTX - hops) // NCTX) % SLOTS
        to = dev(me, halves[piece], hop(-hops))
        return remote(dsum.at[a, piece], own.at[at, piece], dk_ss.at[a, 3 + piece], dk_rs.at[at, 3 + piece], to)

    def pass_back(a):
        for piece in range(2):
            arrived(rx.at[a, piece], dk_rs.at[a, piece])
            dsum[a, piece] = (dko[a, piece] + rx[a, piece].astype(jnp.float32)).astype(jnp.bfloat16)
            owner_copy(a, piece).start()

    def slot(a, carry):
        came(a, 0)

        @pl.when(has_near(a))
        def _():
            came(a, 2)

        @pl.when(has_far(a))
        def _():
            came(a, 4)

        acc[...] = jnp.zeros_like(acc)

        def one(i, carry):
            pair(a, i)

            @pl.when(i == 0)
            def _():
                far_slot(a + 1)

            @pl.when(a == 0)
            def _():
                near_slot(2 + i)

            @pl.when((i == 0) & (a > 0))
            def _():
                pass_back(a - 1)

            return carry

        lax.fori_loop(0, NX // 2, one, 0)
        swap(a)
        return carry

    lax.fori_loop(0, SLOTS, slot, 0)

    for n, to in enumerate((qr, gr)):
        arrived(to.at[:, pl.ds(0, NJ - 1)], q_ss.at[n])
        arrived(kc.at[0, pl.ds(0, (NJ - 1) * SLOTS * ROWS)], a_ss.at[n])

    def sent_keys(a, carry):
        def sent(n):
            arrived(rx.at[a, 0], f_ss.at[a, n])

        sent(0)
        for n, when in ((1, sends_near(a)), (2, has_near(a)), (3, has_near(a) & sends_near(a)), (4, has_far(a))):
            pl.when(when)(functools.partial(sent, n))
        return carry

    lax.fori_loop(0, SLOTS, sent_keys, 0)

    def reduce(a, _):
        for n in (2, 3, 4):
            arrived(rx.at[a, 0], dk_rs.at[a, n])
        total = dko[a, 2] + rx[a, 2].astype(jnp.float32)
        for n in range(2):
            total = total + own[a, n].astype(jnp.float32)
        home[:, a] = total.astype(jnp.bfloat16)
        return _

    def home_src(n, j, at):
        return home.at[n, at, j // 2, pl.ds(pl.multiple_of((j % 2) * ROWS, ROWS), ROWS)]

    def home_dst(n, j, at):
        return (dk_ref, dv_ref)[n].at[at, 0, :, pl.ds(pl.multiple_of(j * HD, HD), HD)]

    def go_home(part):
        lax.fori_loop(2 * part, 2 * part + 2, reduce, 0)
        at = pl.ds(2 * part, 2)
        for p in PEERS:
            j = peer(*p)
            for n in range(2):
                remote(home_src(n, j, at), home_dst(n, me, at), h_ss.at[n], h_rs.at[n], dev(j, y, c)).start()
        for n in range(2):
            pltpu.make_async_copy(home_src(n, me, at), home_dst(n, me, at), h_rs.at[n]).start()

    go_home(0)
    pass_back(SLOTS - 1)
    go_home(1)

    def sent_grads(a, carry):
        for n in range(5):
            arrived(rx.at[a, 0], dk_ss.at[a, n])
        return carry

    lax.fori_loop(0, SLOTS, sent_grads, 0)
    arrived(dqs.at[:, pl.ds(0, NJ - 1)], dq_ss.at[0])
    arrived(dq_ref, dq_rs.at[0])
    for n, ref in enumerate((dk_ref, dv_ref)):
        arrived(kc.at[0, pl.ds(0, (NJ - 1) * SLOTS * ROWS)], h_ss.at[n])
        arrived(ref, h_rs.at[n])


def handed_on(dq, dk, dv, dq_out, dk_out, dv_out, dq_mid, dk_mid, dv_mid, sem):
    parts = [(dq, dq_mid, dq_out, a) for a in range(SLOTS)]
    parts += [(dk, dk_mid, dk_out, pl.ds(0, SLOTS)), (dv, dv_mid, dv_out, pl.ds(0, SLOTS))]
    ins = [pltpu.make_async_copy(r.at[at], m.at[at], sem.at[0, n]) for n, (r, m, _, at) in enumerate(parts)]
    outs = [pltpu.make_async_copy(m.at[at], o.at[at], sem.at[1, n]) for n, (_, m, o, at) in enumerate(parts)]
    for copy in ins:
        copy.start()
    for one, two in zip(ins, outs):
        one.wait()
        two.start()
    for copy in outs:
        copy.wait()


def body(queries, key_vectors, value_vectors, grad_output, doc_ids):
    bf, f32, dma = jnp.bfloat16, jnp.float32, pltpu.SemaphoreType.DMA
    hbm = pl.BlockSpec(memory_space=pltpu.HBM)
    vmem = pltpu.VMEM
    like = jax.ShapeDtypeStruct
    results = pl.pallas_call(
        kernel,
        out_shape=(
            like(queries.shape, bf),
            like(key_vectors.shape, bf),
            like(value_vectors.shape, bf),
        ),
        in_specs=[hbm] * 4 + [pl.BlockSpec(memory_space=vmem)],
        out_specs=(hbm,) * 3,
        scratch_shapes=[
            vmem((SLOTS, NJ, ROWS, QW), bf),
            vmem((SLOTS, NJ, ROWS, QW), bf),
            vmem((SLOTS, NJ, ROWS, QW), bf),
            vmem((2, SLOTS, 3, NX, 2, GRP, HD), bf),
            vmem((2, STACK, HD), bf),
            vmem((2, STACK, HD), bf),
            vmem((2, NKEY, HD), bf),
            vmem((2, NKEY, HD), bf),
            vmem((2, NKEY, HD), f32),
            vmem((NKEY, HD), f32),
            vmem((HD, HD), jnp.int32),
            vmem((2, 24, GRP, HD), f32),
            vmem((SLOTS, 3, 2, NX, GRP, HD), bf),
            vmem((SLOTS, 3, 2, NX, GRP, HD), f32),
            vmem((SLOTS, 3, 2, NX, GRP, HD), bf),
            vmem((SLOTS, 2, 2, NX, GRP, HD), bf),
            vmem((SLOTS, 2, 2, NX, GRP, HD), bf),
            vmem((2, SLOTS, NX, GRP, HD), bf),
            dma((2,)),
            dma((2, SLOTS, NJ)),
            dma((2,)),
            dma((2,)),
            dma((SLOTS, 5)),
            dma((SLOTS, 5)),
            dma((1,)),
            dma((1,)),
            dma((SLOTS, 5)),
            dma((SLOTS, 5)),
            dma((2,)),
            dma((2,)),
            pltpu.SemaphoreType.REGULAR,
        ],
        compiler_params=pltpu.CompilerParams(
            collective_id=0, has_side_effects=True, vmem_limit_bytes=62 << 20
        ),
    )(queries, key_vectors, value_vectors, grad_output, doc_ids.reshape(HD, HD))
    return pl.pallas_call(
        handed_on,
        out_shape=tuple(like(r.shape, bf) for r in results),
        in_specs=[hbm] * 3,
        out_specs=(hbm,) * 3,
        scratch_shapes=[vmem(r.shape, bf) for r in results] + [dma((2, 6))],
    )(*results)


def solution(mesh):
    placed = P(None, "ctx", "head", None)
    return jax.shard_map(
        body,
        mesh=mesh,
        in_specs=(placed,) * 4 + (P(),),
        out_specs=(placed,) * 3,
        check_vma=False,
    )
```

```python
import functools
import math

import jax
import jax.numpy as jnp
from jax import lax
from jax.experimental import pallas as pl
from jax.experimental.pallas import tpu as pltpu
from jax.sharding import PartitionSpec as P

MESH = pl.DeviceIdType.MESH
HD = 128
NX = 4
NJ = 8
NCTX = 16
NZ = 8
SLOTS = 4
ROWS = 16
GRP = 32
HPG = 12
QW = HPG * HD
NKEY = 17 * GRP
STACK = HPG * GRP
HOLD = 2
LOG2E = 1.4426950408889634
FACTOR = 1.0 / math.sqrt(HD)
PEERS = tuple((dx, dc) for dx in (2, 1, 3, 0) for dc in (0, 1) if (dx, dc) != (0, 0))


def kernel(
    q_ref, k_ref, v_ref, g_ref, doc_ref, dq_ref, dk_ref, dv_ref,
    qr, gr, dqs, kv, qc, gc, kc, vc, bias, band, start, acc, dks, dko, rx, dsum, own, home,
    q_ss, q_rs, a_ss, a_rs, f_ss, f_rs, dq_ss, dq_rs, dk_ss, dk_rs, h_ss, h_rs, met,
):
    head = lax.axis_index("head")
    c = lax.axis_index("ctx")
    x, y, core = head // 4, (head // 2) % 2, head % 2
    me = x * 2 + core
    other = 1 - y

    def dev(nj, ny, nc):
        return dict(head=(nj // 2) * 4 + ny * 2 + nj % 2, ctx=nc)

    def hop(by):
        return (c + by + NCTX) % NCTX

    def peer(dx, dc):
        return ((x + dx) % NX) * 2 + (core + dc) % 2

    def remote(src, dst, ss, rs, to):
        return pltpu.make_async_remote_copy(
            src_ref=src, dst_ref=dst, send_sem=ss, recv_sem=rs, device_id=to, device_id_type=MESH
        )

    def arrived(ref, sem):
        pltpu.make_async_copy(ref, ref, sem).wait()

    z = c % NZ
    barrier = pltpu.get_barrier_semaphore()
    over = dev(me, other, c)
    after = dev(me, (y + (z + 1) // NZ) % 2, hop(1))

    def announce(to):
        pl.semaphore_signal(barrier, inc=1, device_id=to, device_id_type=MESH)

    for dx in range(1, NX):
        announce(dev(((x + dx) % NX) * 2, y, c))

    @pl.when(core == 1)
    def _():
        announce(dev(2 * x, y, c))

    y_before, y_two = (y + 1 - (z + NZ - 1) // NZ) % 2, (y + (z + 2) // NZ) % 2
    for ny, by in ((other, 0), ((y + (z + 1) // NZ) % 2, 1), (y_before, -1), (y_two, 2)):
        announce(dev(2 * x + 1, ny, hop(by)))

    def tell(sem):
        pl.semaphore_signal(sem, inc=1, device_id=dev(2 * x + 1 - core, y, c), device_id_type=MESH)

    @pl.when(core == 0)
    def _():
        pl.semaphore_wait(barrier, NJ - 1)
        tell(met)

    @pl.when(core == 1)
    def _():
        pl.semaphore_wait(met, 1)

    def kv_src(ref, j):
        return ref.at[:, 0, :, pl.ds(pl.multiple_of(j * HD, HD), HD)]

    def kv_dst(n, j):
        return kv.at[n, :, 2, j // 2, y, pl.ds(pl.multiple_of((j % 2) * ROWS, ROWS), ROWS)]

    for p in PEERS:
        j = peer(*p)
        for n, ref in enumerate((k_ref, v_ref)):
            remote(kv_src(ref, j), kv_dst(n, me), a_ss.at[n], a_rs.at[n], dev(j, y, c)).start()
    for n, ref in enumerate((k_ref, v_ref)):
        pltpu.make_async_copy(kv_src(ref, me), kv_dst(n, me), a_rs.at[n]).start()

    def q_src(ref, a, j):
        return ref.at[a, 0, :, pl.ds(pl.multiple_of(j * QW, QW), QW)]

    def send_q(a):
        for p in PEERS:
            j = peer(*p)
            for n, (ref, to) in enumerate(((q_ref, qr), (g_ref, gr))):
                remote(q_src(ref, a, j), to.at[a, me], q_ss.at[n], q_rs.at[n, a, me], dev(j, y, c)).start()
        for n, (ref, to) in enumerate(((q_ref, qr), (g_ref, gr))):
            pltpu.make_async_copy(q_src(ref, a, me), to.at[a, me], q_rs.at[n, a, me]).start()

    send_q(0)

    send_q(1)

    for n in range(2):
        arrived(kv.at[n, :, 2, :, y], a_rs.at[n])
    step = (c + 1) // NCTX
    halves = ((y + 1 - (z + NZ - 2) // NZ) % 2, (y + 1 - (z + NZ - 1) // NZ) % 2, y)

    def half(a, piece, of):
        return kv.at[:, a, piece, :, halves[of]]

    for first, piece in ((0, 0), (0, 1), (1, 0)):

        @pl.when(c == first)
        def _(piece=piece):
            kv[:, 0, piece] = jnp.zeros((2, NX, 2, GRP, HD), jnp.bfloat16)

    def sends_near(a):
        return (c < NCTX - 1) | (a < SLOTS - 1)

    def has_near(a):
        return (c > 0) | (a > 0)

    def has_far(a):
        return (c > 1) | (a > 0)

    def own_over(a):
        return remote(half(a, 2, 2), half(a, 2, 2), f_ss.at[a, 0], f_rs.at[a, 0], over)

    def own_after(a):
        at = (a + step) % SLOTS
        return remote(half(a, 2, 2), half(at, 1, 2), f_ss.at[a, 1], f_rs.at[at, 1], after)

    def near_after(a):
        at = (a + step) % SLOTS
        return remote(half(a, 1, 1), half(at, 0, 1), f_ss.at[a, 3], f_rs.at[at, 3], after)

    def near_over(a):
        return remote(half(a, 1, 1), half(a, 1, 1), f_ss.at[a, 2], f_rs.at[a, 2], over)

    def far_over(a):
        return remote(half(a, 0, 0), half(a, 0, 0), f_ss.at[a, 4], f_rs.at[a, 4], over)

    def came(a, n):
        arrived(rx.at[a, 0], f_rs.at[a, n])

    @pl.when(core == 1)
    def _():
        pl.semaphore_wait(barrier, 8)
        tell(met)

    @pl.when(core == 0)
    def _():
        pl.semaphore_wait(met, 1)

    def own_slot(a):
        @pl.when(sends_near(a))
        def _():
            own_after(a).start()

        own_over(a).start()

    def near_slot(a):
        @pl.when(has_near(a))
        def _():
            came(a, 1)

            @pl.when(sends_near(a))
            def _():
                near_after(a).start()

            near_over(a).start()

    def far_slot(a):
        @pl.when((a < SLOTS) & has_far(a))
        def _():
            came(a, 3)
            far_over(a).start()

    own_slot(0)
    own_slot(1)
    send_q(2)
    send_q(3)

    doc = doc_ref[...]
    row = lax.broadcasted_iota(jnp.int32, doc.shape, 0)
    lane = lax.broadcasted_iota(jnp.int32, doc.shape, 1)
    before = pltpu.roll(doc, 1, 1)
    before = jnp.where(lane == 0, pltpu.roll(before, 1, 0), before)
    run = jnp.where(doc != before, row * HD + lane, 0)
    for s in (1, 2, 4, 8, 16, 32, 64):
        run = jnp.maximum(run, jnp.where(lane >= s, pltpu.roll(run, s, 1), 0))
    last = jnp.broadcast_to(jnp.max(run, axis=1, keepdims=True), doc.shape)
    carry = jnp.where(row >= 1, pltpu.roll(last, 1, 0), 0)
    for s in (1, 2, 4, 8, 16, 32, 64):
        carry = jnp.maximum(carry, jnp.where(row >= s, pltpu.roll(carry, s, 0), 0))
    start[...] = jnp.maximum(run, carry)

    near_slot(0)
    own_slot(2)
    near_slot(1)
    far_slot(0)
    own_slot(3)

    key_at = lax.broadcasted_iota(jnp.int32, (NKEY, HD), 0)
    lane8 = lax.broadcasted_iota(jnp.int32, (8, HD), 1)
    ahead = key_at - lax.broadcasted_iota(jnp.int32, (NKEY, HD), 1) % GRP
    band[...] = jnp.where((ahead > 0) & (ahead <= 512), 0.0, -1e30)

    def dq_dst(a, j):
        return dq_ref.at[a, 0, :, pl.ds(pl.multiple_of(j * QW, QW), QW)]

    def send_dq(a, xs):
        for nc in range(2):
            j = 2 * xs + nc

            @pl.when(j == me)
            def _(j=j):
                pltpu.make_async_copy(dqs.at[a, j], dq_dst(a, me), dq_rs.at[0]).start()

            @pl.when(j != me)
            def _(j=j):
                remote(dqs.at[a, j], dq_dst(a, me), dq_ss.at[0], dq_rs.at[0], dev(j, y, c)).start()

    def held_dq():
        def each(n, carry):
            send_dq(n % HOLD, (x + 2 + 3 * (n // HOLD)) % NX)
            return carry

        lax.fori_loop(0, HOLD * NX, each, 0)

    def await_chunk(a, i):
        xs = (x + 2 * (i % 2) + i // 2) % NX
        for nc in range(2):
            for n, to in enumerate((qr, gr)):
                arrived(to.at[a, 2 * xs + nc], q_rs.at[n, a, 2 * xs + nc])
        return xs

    def chunk(a, xs, qc, gc, kc, vc, bias):
        off = 2 * xs + y
        for h in range(HPG):
            at = pl.ds(h * HD, HD)
            qc[pl.ds(h * GRP, GRP), :] = qr[a, pl.ds(2 * xs, 2), :, at].reshape(GRP, HD)
            gc[pl.ds(h * GRP, GRP), :] = gr[a, pl.ds(2 * xs, 2), :, at].reshape(GRP, HD)
        for t in range(17):
            at = off + t
            kc[pl.ds(t * GRP, GRP), :] = kv[0, a, at // 8, (at % 8) // 2, at % 2]
            vc[pl.ds(t * GRP, GRP), :] = kv[1, a, at // 8, (at % 8) // 2, at % 2]
        first = (a * NCTX + c) * 256 + off * GRP
        line = jnp.broadcast_to(start[pl.ds((a * NCTX + c) * 2 + off // 4, 1), :], (8, HD))
        line = pltpu.roll(line, (HD - GRP * (off % 4)) % HD, 1)
        line = jnp.where(lane8 < GRP, line, 0)
        line = line + pltpu.roll(line, GRP, 1)
        line = line + pltpu.roll(line, 2 * GRP, 1)
        bias[...] = jnp.where(key_at >= (line - (first - 512))[:1], band[...], -1e30)
        nt = (((1,), (1,)), ((), ()))
        scores = lax.dot_general(kc[...], qc[...], nt, preferred_element_type=jnp.float32)
        dweights = lax.dot_general(vc[...], gc[...], nt, preferred_element_type=jnp.float32)
        both = jnp.concatenate([bias[...]] * (STACK // HD), axis=1)
        scaled = scores * (FACTOR * LOG2E) + both
        top = jnp.max(scaled, axis=0, keepdims=True)
        exponent = jnp.exp2(scaled - top)
        total = jnp.sum(exponent, axis=0, keepdims=True)
        cross = jnp.sum(exponent * dweights, axis=0, keepdims=True)
        inverse = 1.0 / total
        weights = exponent * inverse
        dscores = (weights * (dweights - cross * inverse)).astype(jnp.bfloat16)
        weights = weights.astype(jnp.bfloat16)
        nn = (((1,), (0,)), ((), ()))
        dv = lax.dot_general(weights, gc[...], nn, preferred_element_type=jnp.float32)
        dk = lax.dot_general(dscores, qc[...], nn, preferred_element_type=jnp.float32)
        tn = (((0,), (0,)), ((), ()))
        dq = lax.dot_general(dscores, kc[...], tn, preferred_element_type=jnp.float32)
        acc[0, pl.ds(off, 17)] += dk.reshape(17, GRP, HD)
        acc[1, pl.ds(off, 17)] += dv.reshape(17, GRP, HD)
        dq = (dq * FACTOR).astype(jnp.bfloat16)
        for h in range(HPG):
            dqs[a, pl.ds(2 * xs, 2), :, pl.ds(h * HD, HD)] = dq[h * GRP : (h + 1) * GRP].reshape(2, ROWS, HD)

    def pair(a, i):
        both = [await_chunk(a, 2 * i), await_chunk(a, 2 * i + 1)]
        pl.when((a == HOLD) & (i == 0))(held_dq)
        for n, xs in enumerate(both):
            chunk(a, xs, *[ref.at[n] for ref in (qc, gc, kc, vc, bias)])
        for xs in both:
            pl.when(a >= HOLD)(functools.partial(send_dq, a, xs))

    def swap_copy(a, piece):
        return remote(dks.at[a, piece], rx.at[a, piece], dk_ss.at[a, piece], dk_rs.at[a, piece], over)

    def swap(a):
        for piece in range(3):
            for n, scale in enumerate((FACTOR, 1.0)):
                for xx in range(NX):
                    at = piece * 8 + 2 * xx
                    dko[a, piece, n, xx] = acc[n, at + halves[piece]] * scale
                    dks[a, piece, n, xx] = (acc[n, at + 1 - halves[piece]] * scale).astype(jnp.bfloat16)
            swap_copy(a, piece).start()

    def owner_copy(a, piece):
        hops = 2 - piece
        at = (a + SLOTS - 1 + (c + NCTX - hops) // NCTX) % SLOTS
        to = dev(me, halves[piece], hop(-hops))
        return remote(dsum.at[a, piece], own.at[at, piece], dk_ss.at[a, 3 + piece], dk_rs.at[at, 3 + piece], to)

    def pass_back(a):
        for piece in range(2):
            arrived(rx.at[a, piece], dk_rs.at[a, piece])
            dsum[a, piece] = (dko[a, piece] + rx[a, piece].astype(jnp.float32)).astype(jnp.bfloat16)
            owner_copy(a, piece).start()

    def slot(a, carry):
        came(a, 0)

        @pl.when(has_near(a))
        def _():
            came(a, 2)

        @pl.when(has_far(a))
        def _():
            came(a, 4)

        acc[...] = jnp.zeros_like(acc)

        def one(i, carry):
            pair(a, i)

            @pl.when(i == 0)
            def _():
                far_slot(a + 1)

            @pl.when(a == 0)
            def _():
                near_slot(2 + i)

            @pl.when((i == 0) & (a > 0))
            def _():
                pass_back(a - 1)

            return carry

        lax.fori_loop(0, NX // 2, one, 0)
        swap(a)
        return carry

    lax.fori_loop(0, SLOTS, slot, 0)

    for n, to in enumerate((qr, gr)):
        arrived(to.at[:, pl.ds(0, NJ - 1)], q_ss.at[n])
        arrived(kc.at[0, pl.ds(0, (NJ - 1) * SLOTS * ROWS)], a_ss.at[n])

    def sent_keys(a, carry):
        def sent(n):
            arrived(rx.at[a, 0], f_ss.at[a, n])

        sent(0)
        for n, when in ((1, sends_near(a)), (2, has_near(a)), (3, has_near(a) & sends_near(a)), (4, has_far(a))):
            pl.when(when)(functools.partial(sent, n))
        return carry

    lax.fori_loop(0, SLOTS, sent_keys, 0)

    def reduce(a, _):
        for n in (2, 3, 4):
            arrived(rx.at[a, 0], dk_rs.at[a, n])
        total = dko[a, 2] + rx[a, 2].astype(jnp.float32)
        for n in range(2):
            total = total + own[a, n].astype(jnp.float32)
        home[:, a] = total.astype(jnp.bfloat16)
        return _

    def home_src(n, j, at):
        return home.at[n, at, j // 2, pl.ds(pl.multiple_of((j % 2) * ROWS, ROWS), ROWS)]

    def home_dst(n, j, at):
        return (dk_ref, dv_ref)[n].at[at, 0, :, pl.ds(pl.multiple_of(j * HD, HD), HD)]

    def go_home(part):
        lax.fori_loop(2 * part, 2 * part + 2, reduce, 0)
        at = pl.ds(2 * part, 2)
        for p in PEERS:
            j = peer(*p)
            for n in range(2):
                remote(home_src(n, j, at), home_dst(n, me, at), h_ss.at[n], h_rs.at[n], dev(j, y, c)).start()
        for n in range(2):
            pltpu.make_async_copy(home_src(n, me, at), home_dst(n, me, at), h_rs.at[n]).start()

    go_home(0)
    pass_back(SLOTS - 1)
    go_home(1)

    def sent_grads(a, carry):
        for n in range(5):
            arrived(rx.at[a, 0], dk_ss.at[a, n])
        return carry

    lax.fori_loop(0, SLOTS, sent_grads, 0)
    arrived(dqs.at[:, pl.ds(0, NJ - 1)], dq_ss.at[0])
    arrived(dq_ref, dq_rs.at[0])
    for n, ref in enumerate((dk_ref, dv_ref)):
        arrived(kc.at[0, pl.ds(0, (NJ - 1) * SLOTS * ROWS)], h_ss.at[n])
        arrived(ref, h_rs.at[n])


def handed_on(dq, dk, dv, dq_out, dk_out, dv_out, dq_mid, dk_mid, dv_mid, sem):
    parts = [(dq, dq_mid, dq_out, a) for a in range(SLOTS)]
    parts += [(dk, dk_mid, dk_out, pl.ds(0, SLOTS)), (dv, dv_mid, dv_out, pl.ds(0, SLOTS))]
    ins = [pltpu.make_async_copy(r.at[at], m.at[at], sem.at[0, n]) for n, (r, m, _, at) in enumerate(parts)]
    outs = [pltpu.make_async_copy(m.at[at], o.at[at], sem.at[1, n]) for n, (_, m, o, at) in enumerate(parts)]
    for copy in ins:
        copy.start()
    for one, two in zip(ins, outs):
        one.wait()
        two.start()
    for copy in outs:
        copy.wait()


def body(queries, key_vectors, value_vectors, grad_output, doc_ids):
    bf, f32, dma = jnp.bfloat16, jnp.float32, pltpu.SemaphoreType.DMA
    hbm = pl.BlockSpec(memory_space=pltpu.HBM)
    vmem = pltpu.VMEM
    like = jax.ShapeDtypeStruct
    results = pl.pallas_call(
        kernel,
        out_shape=(
            like(queries.shape, bf),
            like(key_vectors.shape, bf),
            like(value_vectors.shape, bf),
        ),
        in_specs=[hbm] * 4 + [pl.BlockSpec(memory_space=vmem)],
        out_specs=(hbm,) * 3,
        scratch_shapes=[
            vmem((SLOTS, NJ, ROWS, QW), bf),
            vmem((SLOTS, NJ, ROWS, QW), bf),
            vmem((SLOTS, NJ, ROWS, QW), bf),
            vmem((2, SLOTS, 3, NX, 2, GRP, HD), bf),
            vmem((2, STACK, HD), bf),
            vmem((2, STACK, HD), bf),
            vmem((2, NKEY, HD), bf),
            vmem((2, NKEY, HD), bf),
            vmem((2, NKEY, HD), f32),
            vmem((NKEY, HD), f32),
            vmem((HD, HD), jnp.int32),
            vmem((2, 24, GRP, HD), f32),
            vmem((SLOTS, 3, 2, NX, GRP, HD), bf),
            vmem((SLOTS, 3, 2, NX, GRP, HD), f32),
            vmem((SLOTS, 3, 2, NX, GRP, HD), bf),
            vmem((SLOTS, 2, 2, NX, GRP, HD), bf),
            vmem((SLOTS, 2, 2, NX, GRP, HD), bf),
            vmem((2, SLOTS, NX, GRP, HD), bf),
            dma((2,)),
            dma((2, SLOTS, NJ)),
            dma((2,)),
            dma((2,)),
            dma((SLOTS, 5)),
            dma((SLOTS, 5)),
            dma((1,)),
            dma((1,)),
            dma((SLOTS, 5)),
            dma((SLOTS, 5)),
            dma((2,)),
            dma((2,)),
            pltpu.SemaphoreType.REGULAR,
        ],
        compiler_params=pltpu.CompilerParams(
            collective_id=0, has_side_effects=True, vmem_limit_bytes=62 << 20
        ),
    )(queries, key_vectors, value_vectors, grad_output, doc_ids.reshape(HD, HD))
    return pl.pallas_call(
        handed_on,
        out_shape=tuple(like(r.shape, bf) for r in results),
        in_specs=[hbm] * 3,
        out_specs=(hbm,) * 3,
        scratch_shapes=[vmem(r.shape, bf) for r in results] + [dma((2, 6))],
    )(*results)


def solution(mesh):
    placed = P(None, "ctx", "head", None)
    return jax.shard_map(
        body,
        mesh=mesh,
        in_specs=(placed,) * 4 + (P(),),
        out_specs=(placed,) * 3,
        check_vma=False,
    )
```
